32 devices in a mesh: grp: 4 (over x, core), seq: 8 (over z, y).
Axes of the slice: x: 2, y: 2, z: 4, core: 2. Of those that a mesh axis runs over, the one named last changes fastest.
Arguments:
- signal: bfloat16 [4, 1024, 2048], P('grp', 'seq'), may hold values from -6 to 6
- gate_in: bfloat16 [4, 1024, 2048], P('grp', 'seq'), may hold values from -6 to 6
- gate_out: bfloat16 [4, 1024, 2048], P('grp', 'seq'), may hold values from -6 to 6
- pos_weight: float32 [33, 64], replicated, may hold values from -1 to 1
- pos_bias: float32 [64], replicated, may hold values from -1 to 1
- inner_weight: float32 [2, 64, 64], replicated, may hold values from -0.75 to 0.75
- inner_bias: float32 [2, 64], replicated, may hold values from -1 to 1
- frequency: float32 [64], replicated, may hold values from 1 to 12
- out_weight: float32 [64, 2048], replicated, may hold values from -0.75 to 0.75
- decay_rates: float32 [2048], replicated, may hold values from 0.3 to 3000
- skip_gain: float32 [2048], replicated, may hold values from -6 to 6
Outputs:
- layer_out: bfloat16 [4, 1024, 2048], P('grp', 'seq')
The draws below stay inside these ranges and needn't reach their ends.
All inputs are finite; a program needn't handle non-finite values.
Results may differ from the reference program's by a relative error of at most 0.009.
Values may be sent and summed in bfloat16 or wider, within the bound.
A program may use at most 64 MiB of HBM per device.

```python
import math
import jax
import jax.numpy as jnp
from jax import lax

D = 2048
ORDER = 64
EMB = 33
INNER = 2
POS_DEV = 128
SEQS = 4
SEQ = 1024
N_SEQ = 8


def level_of(own_key, shape, cuts, smallest, largest):
    def one(position, blocks):
        heights = jax.random.uniform(jax.random.fold_in(jax.random.fold_in(own_key, 6), position), (blocks,), jnp.float32, smallest / len(cuts), largest / len(cuts))
        return jnp.repeat(jnp.exp(heights), shape[position] // blocks).reshape((-1,) + (1,) * (len(shape) - position - 1))

    factor_of = one(*cuts[0])
    for cut in cuts[1:]:
        factor_of = factor_of * one(*cut)
    return factor_of


def bell_draw(own_key, extent, scale, limit, cuts=(), kind=jnp.bfloat16):
    values = scale * jax.random.normal(own_key, extent, jnp.float32)
    if cuts:
        values = values * level_of(own_key, extent, cuts, -0.22, 0.18)
    return jnp.clip(values, -limit, limit).astype(kind)


def setup_inputs(seed: int = 0) -> dict:
    arg_keys = jax.random.split(jax.random.key(seed), 12)
    signal = bell_draw(arg_keys[0], (SEQS, SEQ, D), 1.0, 6.0, ((0, 4), (1, 8)))
    gate_in = bell_draw(arg_keys[1], (SEQS, SEQ, D), 1.0, 6.0, ((0, 4), (1, 8)))
    gate_out = bell_draw(arg_keys[2], (SEQS, SEQ, D), 1.0, 6.0, ((0, 4), (1, 8)))
    pos_weight = bell_draw(arg_keys[3], (EMB, ORDER), EMB ** -0.5, 1.0, (), jnp.float32)
    pos_bias = jnp.clip(jax.random.uniform(arg_keys[4], (ORDER,), jnp.float32, -1.0, 1.0), -1.0, 1.0)
    inner_weight = bell_draw(arg_keys[5], (INNER, ORDER, ORDER), ORDER ** -0.5, 0.75, (), jnp.float32)
    inner_bias = jnp.clip(jax.random.uniform(arg_keys[6], (INNER, ORDER), jnp.float32, -1.0, 1.0), -1.0, 1.0)
    frequency = jnp.clip(jnp.exp(jax.random.uniform(arg_keys[7], (ORDER,), jnp.float32, math.log(1.0), math.log(12.0))), 1.0, 12.0)
    out_weight = bell_draw(arg_keys[8], (ORDER, D), ORDER ** -0.5, 0.75, (), jnp.float32)
    decay_rates = jnp.clip(jnp.exp(jax.random.uniform(arg_keys[9], (D,), jnp.float32, math.log(0.3), math.log(3000.0))), 0.3, 3000.0)
    skip_gain = bell_draw(arg_keys[10], (D,), 1.0, 6.0, (), jnp.float32)
    return dict(signal=signal, gate_in=gate_in, gate_out=gate_out, pos_weight=pos_weight, pos_bias=pos_bias, inner_weight=inner_weight, inner_bias=inner_bias, frequency=frequency, out_weight=out_weight, decay_rates=decay_rates, skip_gain=skip_gain)


TWO_PI = 6.283185307179586
FLOOR_SHIFT = 0.05
EPSILON = 1e-06
HIGHEST = lax.Precision.HIGHEST

def unit_angle(index, period):
    return (index % period).astype(jnp.float32) * (TWO_PI / period)

def section_tables(row_ids, col_ids, period):
    angle = unit_angle(row_ids[:, None] * col_ids[None, :], period)
    return (jnp.cos(angle).astype(jnp.bfloat16), jnp.sin(angle).astype(jnp.bfloat16))

def filter_rows(positions, total, pos_weight, pos_bias, inner_weight, inner_bias, frequency, out_weight, decay_rates):
    band_count = (pos_weight.shape[0] - 1) // 2
    position_f = positions.astype(jnp.float32)
    moments = position_f / (total - 1)
    phases = position_f * (TWO_PI / total)
    tone_list = jnp.linspace(0.0001, band_count - 1, band_count).astype(jnp.float32)
    angles = tone_list[:, None] * phases[None, :]
    features = jnp.concatenate([moments[None, :], jnp.cos(angles), -jnp.sin(angles)], axis=0)
    hidden = jnp.sin(frequency[:, None] * (jnp.dot(pos_weight.T, features, precision=HIGHEST) + pos_bias[:, None]))
    for layer_index in range(inner_weight.shape[0]):
        hidden = jnp.sin(frequency[:, None] * (jnp.dot(inner_weight[layer_index].T, hidden, precision=HIGHEST) + inner_bias[layer_index][:, None]))
    shaped = lax.dot_general(hidden, out_weight, (((0,), (0,)), ((), ())), precision=HIGHEST)
    return shaped * (jnp.exp(-moments[:, None] * decay_rates[None, :]) + FLOOR_SHIFT)

def forward_first(source, fwd_cos, fwd_sin, blocks, rows_freq):
    span = source.shape[0] // blocks
    width = source.shape[1]
    flat = source.reshape(blocks, span * width)
    real_part = jnp.dot(fwd_cos, flat, preferred_element_type=jnp.float32)
    imag_part = -jnp.dot(fwd_sin, flat, preferred_element_type=jnp.float32)
    return (real_part.astype(jnp.bfloat16).reshape(rows_freq, span, width), imag_part.astype(jnp.bfloat16).reshape(rows_freq, span, width))

def row_tables(row_id, span, rows_freq, period):
    column_ids = jnp.arange(span, dtype=jnp.int32)
    return section_tables(row_id + rows_freq * column_ids, column_ids, period)

def forward_row(cosines, sines, part_real, part_imag):
    spec_real = jnp.dot(cosines, part_real, preferred_element_type=jnp.float32) + jnp.dot(sines, part_imag, preferred_element_type=jnp.float32)
    spec_imag = jnp.dot(cosines, part_imag, preferred_element_type=jnp.float32) - jnp.dot(sines, part_real, preferred_element_type=jnp.float32)
    return (spec_real, spec_imag)

def reference(signal, gate_in, gate_out, pos_weight, pos_bias, inner_weight, inner_bias, frequency, out_weight, decay_rates, skip_gain):
    blocks = N_SEQ
    span = POS_DEV
    length = SEQ
    rows_freq = 2 * blocks
    period = 2 * length
    width = signal.shape[2]
    freq_ids = jnp.arange(rows_freq, dtype=jnp.int32)
    block_ids = jnp.arange(blocks, dtype=jnp.int32)
    shaped = filter_rows(jnp.arange(length, dtype=jnp.int32), length, pos_weight, pos_bias, inner_weight, inner_bias, frequency, out_weight, decay_rates)
    scale = lax.rsqrt(lax.optimization_barrier(jnp.sum(shaped * shaped, axis=0)) + EPSILON)
    filter_taps = shaped.astype(jnp.bfloat16)
    fwd_cos, fwd_sin = section_tables(freq_ids, block_ids, rows_freq)
    back_cos, back_sin = section_tables(block_ids, freq_ids, rows_freq)
    taps_real, taps_imag = forward_first(filter_taps, fwd_cos, fwd_sin, blocks, rows_freq)

    def filter_row(pieces):
        part_real, part_imag, row_id = pieces
        cosines, sines = row_tables(row_id, span, rows_freq, period)
        spec_real, spec_imag = forward_row(cosines, sines, part_real, part_imag)
        return (spec_real.astype(jnp.bfloat16), spec_imag.astype(jnp.bfloat16))
    filter_real, filter_imag = lax.map(filter_row, (taps_real, taps_imag, freq_ids))

    def one_sequence(pieces):
        source, gate_first, gate_second = pieces
        gated = (gate_first.astype(jnp.float32) * source.astype(jnp.float32)).astype(jnp.bfloat16)
        part_real, part_imag = forward_first(gated, fwd_cos, fwd_sin, blocks, rows_freq)

        def data_row(entries):
            row_real, row_imag, spec_real, spec_imag, row_id = entries
            cosines, sines = row_tables(row_id, span, rows_freq, period)
            wave_real, wave_imag = forward_row(cosines, sines, row_real, row_imag)
            filt_real = spec_real.astype(jnp.float32)
            filt_imag = spec_imag.astype(jnp.float32)
            prod_real = ((wave_real * filt_real - wave_imag * filt_imag) * scale).astype(jnp.bfloat16)
            prod_imag = ((wave_real * filt_imag + wave_imag * filt_real) * scale).astype(jnp.bfloat16)
            back_real = jnp.dot(cosines.T, prod_real, preferred_element_type=jnp.float32) - jnp.dot(sines.T, prod_imag, preferred_element_type=jnp.float32)
            back_imag = jnp.dot(cosines.T, prod_imag, preferred_element_type=jnp.float32) + jnp.dot(sines.T, prod_real, preferred_element_type=jnp.float32)
            return (back_real.astype(jnp.bfloat16), back_imag.astype(jnp.bfloat16))
        back_real, back_imag = lax.map(data_row, (part_real, part_imag, filter_real, filter_imag, freq_ids))
        flat_real = back_real.reshape(rows_freq, span * width)
        flat_imag = back_imag.reshape(rows_freq, span * width)
        convolved = (jnp.dot(back_cos, flat_real, preferred_element_type=jnp.float32) - jnp.dot(back_sin, flat_imag, preferred_element_type=jnp.float32)) * (1.0 / period)
        convolved = convolved.reshape(length, width)
        mixed = gate_second.astype(jnp.float32) * (convolved + skip_gain[None, :] * gated.astype(jnp.float32))
        return mixed.astype(jnp.bfloat16)
    return lax.map(one_sequence, (signal, gate_in, gate_out))
```

```python
import functools
import math

import jax
import jax.numpy as jnp
import ml_dtypes
import numpy as np
from jax import lax
from jax.experimental import pallas as pl
from jax.experimental.pallas import tpu as pltpu
from jax.sharding import PartitionSpec as P

TWO_PI = 6.283185307179586
FLOOR_SHIFT = 0.05
EPSILON = 1e-06
HIGHEST = lax.Precision.HIGHEST
LANES = 128
MIB = 1024 * 1024


def row_matrices(blocks, span):
    rows_freq = 2 * blocks
    period = rows_freq * span
    ids = np.arange(span, dtype=np.int64)
    wave = np.arange(blocks + 1)[:, None] + rows_freq * ids[None, :]
    turns = (wave[:, :, None] * ids[None, None, :]) % period
    angle = turns.astype(np.float32) * np.float32(TWO_PI / period)
    cosines, sines = np.cos(angle), np.sin(angle)
    upper = np.concatenate([cosines, sines], axis=2)
    lower = np.concatenate([-sines, cosines], axis=2)
    forward = np.concatenate([upper, lower], axis=1).astype(ml_dtypes.bfloat16)
    return forward, np.ascontiguousarray(forward.transpose(0, 2, 1))


def position_features(length, emb):
    band_count = (emb - 1) // 2
    position_f = np.arange(length, dtype=np.float32)
    moments = position_f / np.float32(length - 1)
    phases = position_f * np.float32(TWO_PI / length)
    tones = np.linspace(0.0001, band_count - 1, band_count).astype(np.float32)
    angles = tones[:, None] * phases[None, :]
    return np.concatenate([moments[None, :], np.cos(angles), -np.sin(angles)], axis=0)


def sine(value):
    turns = jnp.round(value * (1.0 / math.pi))
    rest = value - turns * 3.140625
    rest = rest - turns * 9.67502593994140625e-4
    rest = rest - turns * 1.509957990978376432e-7
    parity = turns - 2.0 * jnp.floor(turns * 0.5)
    square = rest * rest
    poly = -2.3889859e-08 * square + 2.7525562e-06
    poly = poly * square - 0.00019840874
    poly = poly * square + 0.0083333310
    poly = poly * square - 0.16666667
    signed = rest - 2.0 * parity * rest
    return signed + signed * (square * poly)


def weighted(terms):
    total = None
    for factor, value in terms:
        if abs(factor) < 1e-9:
            continue
        if abs(factor - 1.0) < 1e-9:
            total = value if total is None else total + value
        elif abs(factor + 1.0) < 1e-9:
            total = -value if total is None else total - value
        else:
            part = value * factor
            total = part if total is None else total + part
    return total


def sections(load, store, blocks):
    half = blocks // 2
    x = [load(a).astype(jnp.float32) for a in range(blocks)]
    plus = {a: x[a] + x[blocks - a] for a in range(1, half)}
    minus = {a: x[a] - x[blocks - a] for a in range(1, half)}
    for c in range(blocks + 1):
        step = math.pi * c / blocks
        even = c % 2 == 0
        on_cos, on_sin = (plus, minus) if even else (minus, plus)
        middle = [(math.cos(step * half), x[half])] if even else []
        real = weighted([(1.0, x[0])] + middle + [(math.cos(step * a), on_cos[a]) for a in on_cos])
        store(c, 0, real.astype(jnp.bfloat16))
        if 0 < c < blocks:
            middle = [] if even else [(-math.sin(step * half), x[half])]
            imag = weighted(middle + [(-math.sin(step * a), on_sin[a]) for a in on_sin])
            store(c, 1, imag.astype(jnp.bfloat16))


def joined(load, store, blocks, factor):
    half = blocks // 2
    real = [load(c, 0) * (factor if c in (0, blocks) else 2.0 * factor) for c in range(blocks + 1)]
    imag = {c: load(c, 1) * (2.0 * factor) for c in range(1, blocks)}
    for a in range(half + 1):
        step = math.pi * a / blocks
        even_cos = weighted([(math.cos(step * c), real[c]) for c in range(0, blocks + 1, 2)])
        odd_cos = weighted([(math.cos(step * c), real[c]) for c in range(1, blocks + 1, 2)])
        even_sin = weighted([(math.sin(step * c), imag[c]) for c in range(2, blocks, 2)])
        odd_sin = weighted([(math.sin(step * c), imag[c]) for c in range(1, blocks, 2)])
        both = even_cos if odd_sin is None else even_cos - odd_sin
        turn = None
        if odd_cos is not None and even_sin is not None:
            turn = odd_cos - even_sin
        elif odd_cos is not None:
            turn = odd_cos
        elif even_sin is not None:
            turn = -even_sin
        store(a, (both if turn is None else both + turn).astype(jnp.bfloat16))
        if 0 < a < half:
            store(blocks - a, (both if turn is None else both - turn).astype(jnp.bfloat16))


def partner(me, mask, count):
    total, bit = 0, 1
    while bit < count:
        digit = (me // bit) % 2
        total = total + bit * ((1 - digit) if mask & bit else digit)
        bit *= 2
    return total


def layer_kernel(
    blocks,
    span,
    own,
    signal,
    gate_in,
    gate_out,
    features,
    pos_weight,
    pos_bias,
    inner_weight,
    inner_bias,
    frequency,
    out_weight,
    decay_rates,
    skip_gain,
    forward_hbm,
    inverse_hbm,
    out,
    forward,
    inverse,
    gated,
    inbox,
    outbox,
    returned,
    hidden,
    taps,
    tap_rows,
    filt,
    data_rows,
    back,
    table_sem,
    send_sem,
    recv_sem,
):
    me = lax.axis_index("seq")
    chunks = own // LANES
    length = blocks * span
    masks = list(range(blocks - 1, 0, -1))
    peers = {mask: partner(me, mask, blocks) for mask in masks}

    barrier = pltpu.get_barrier_semaphore()
    for mask in masks:
        pl.semaphore_signal(
            barrier, inc=1, device_id={"seq": peers[mask]}, device_id_type=pl.DeviceIdType.MESH
        )
    tables = [
        pltpu.make_async_copy(forward_hbm, forward, table_sem.at[0]),
        pltpu.make_async_copy(inverse_hbm, inverse, table_sem.at[1]),
    ]
    for copy in tables:
        copy.start()

    for chunk in range(chunks):
        for owner in range(blocks):
            columns = pl.ds(owner * own + chunk * LANES, LANES)
            gated[owner, chunk] = (
                gate_in[0, :, columns].astype(jnp.float32)
                * signal[0, :, columns].astype(jnp.float32)
            ).astype(jnp.bfloat16)
    pl.semaphore_wait(barrier, len(masks))

    def exchange(phase, chunk, source_of, target):
        copies = []
        for mask in masks:
            copy = pltpu.make_async_remote_copy(
                src_ref=source_of(peers[mask]),
                dst_ref=target.at[chunk, me],
                send_sem=send_sem.at[phase, chunk, mask],
                recv_sem=recv_sem.at[phase, chunk, mask],
                device_id={"seq": peers[mask]},
                device_id_type=pl.DeviceIdType.MESH,
            )
            copy.start()
            copies.append(copy)
        return copies

    incoming = [
        exchange(0, chunk, lambda peer, chunk=chunk: gated.at[peer, chunk], inbox)
        for chunk in range(chunks)
    ]
    for chunk in range(chunks):
        inbox[chunk, me] = gated[me, chunk]

    order = frequency.shape[1]
    diagonal = lax.broadcasted_iota(jnp.int32, (order, order), 0) == lax.broadcasted_iota(
        jnp.int32, (order, order), 1
    )

    def as_column(row):
        return jnp.sum(jnp.where(diagonal, row, 0.0), axis=1, keepdims=True)

    def layer(weight, values, bias):
        product = lax.dot_general(
            weight,
            values,
            (((0,), (0,)), ((), ())),
            precision=HIGHEST,
            preferred_element_type=jnp.float32,
        )
        return sine(rate * (product + as_column(bias)))

    rate = as_column(frequency[...])
    hidden[...] = layer(pos_weight[...], features[...], pos_bias[...])
    for index in range(inner_weight.shape[0]):
        hidden[...] = layer(inner_weight[index], hidden[...], inner_bias[pl.ds(index, 1), :])
    mine = pl.ds(pl.multiple_of(me * own, LANES), own)
    weight = out_weight[:, mine]
    decay = decay_rates[:, mine]
    energy = jnp.zeros((1, own), jnp.float32)
    for a in range(blocks):
        place = lax.broadcasted_iota(jnp.int32, (span, own), 0) + a * span
        moment = place.astype(jnp.float32) / float(length - 1)
        raw = lax.dot_general(
            hidden[:, a * span : (a + 1) * span],
            weight,
            (((0,), (0,)), ((), ())),
            precision=HIGHEST,
            preferred_element_type=jnp.float32,
        ) * (jnp.exp(-moment * decay) + FLOOR_SHIFT)
        energy = energy + jnp.sum(raw * raw, axis=0, keepdims=True)
        taps[a] = raw.astype(jnp.bfloat16)
    scale = lax.rsqrt(energy + EPSILON)

    group = 16

    def tap_section(step, carry):
        rows = pl.ds(pl.multiple_of(step * group, group), group)

        def store(c, part, value):
            tap_rows[c, part, rows, :] = value

        sections(lambda a: taps[a, rows, :], store, blocks)
        return carry

    lax.fori_loop(0, span // group, tap_section, 0)
    for copy in tables:
        copy.wait()

    def spectrum(c, rows):
        if c in (0, blocks):
            table, data = forward[c, :, :span], rows[0]
        else:
            table, data = forward[c], jnp.concatenate([rows[0], rows[1]], axis=0)
        return jnp.dot(table, data, preferred_element_type=jnp.float32)

    for c in range(blocks + 1):
        filt[c] = spectrum(c, tap_rows.at[c]) * scale

    outgoing = []
    for chunk in range(chunks):
        for copy in incoming[chunk]:
            copy.wait_recv()

        def data_section(step, carry):
            rows = pl.ds(pl.multiple_of(step * group, group), group)

            def store(c, part, value):
                data_rows[c, part, rows, :] = value

            sections(lambda a: inbox[chunk, a, rows, :], store, blocks)
            return carry

        lax.fori_loop(0, span // group, data_section, 0)
        lanes = slice(chunk * LANES, (chunk + 1) * LANES)
        for c in range(blocks + 1):
            wave = spectrum(c, data_rows.at[c])
            wave_real, wave_imag = wave[:span], wave[span:]
            filt_real, filt_imag = filt[c, :span, lanes], filt[c, span:, lanes]
            product = jnp.concatenate(
                [
                    (wave_real * filt_real - wave_imag * filt_imag).astype(jnp.bfloat16),
                    (wave_real * filt_imag + wave_imag * filt_real).astype(jnp.bfloat16),
                ],
                axis=0,
            )
            if c in (0, blocks):
                back[c, :span] = jnp.dot(
                    inverse[c, :span, :], product, preferred_element_type=jnp.float32
                )
            else:
                back[c] = jnp.dot(inverse[c], product, preferred_element_type=jnp.float32)

        def join_section(step, carry):
            small = 8

            def load(c, part):
                return back[c, pl.ds(pl.multiple_of(part * span + step * group, small), group), :]

            def store(a, value):
                outbox[chunk, a, pl.ds(pl.multiple_of(step * group, group), group), :] = value

            joined(load, store, blocks, 1.0 / (2 * length))
            return carry

        lax.fori_loop(0, span // group, join_section, 0)
        outgoing.append(
            exchange(1, chunk, lambda peer, chunk=chunk: outbox.at[chunk, peer], returned)
        )

    def finish(chunk, owner, convolved):
        columns = pl.ds(pl.multiple_of(owner * own + chunk * LANES, LANES), LANES)
        out[0, :, columns] = (
            gate_out[0, :, columns].astype(jnp.float32)
            * (
                convolved.astype(jnp.float32)
                + skip_gain[:, columns] * gated[owner, chunk].astype(jnp.float32)
            )
        ).astype(jnp.bfloat16)

    for chunk in range(chunks):
        finish(chunk, me, outbox[chunk, me])
    for chunk in range(chunks):
        for mask, copy in reversed(list(zip(masks, outgoing[chunk]))):
            copy.wait_recv()
            finish(chunk, peers[mask], returned[chunk, peers[mask]])
    for copies in incoming + outgoing:
        for copy in copies:
            copy.wait_send()


def fused(
    signal,
    gate_in,
    gate_out,
    pos_weight,
    pos_bias,
    inner_weight,
    inner_bias,
    frequency,
    out_weight,
    decay_rates,
    skip_gain,
):
    blocks = lax.axis_size("seq")
    span, width = signal.shape[1], signal.shape[2]
    own = width // blocks
    chunks = own // LANES
    length = span * blocks
    order = frequency.shape[0]
    forward, inverse = row_matrices(blocks, span)
    features = position_features(length, pos_weight.shape[0])
    vmem = pl.BlockSpec(memory_space=pltpu.VMEM)
    anywhere = pl.BlockSpec(memory_space=pl.ANY)
    bf16, f32 = jnp.bfloat16, jnp.float32
    return pl.pallas_call(
        functools.partial(layer_kernel, blocks, span, own),
        out_shape=jax.ShapeDtypeStruct(signal.shape, bf16),
        in_specs=[vmem] * 12 + [anywhere] * 2,
        out_specs=vmem,
        scratch_shapes=[
            pltpu.VMEM(forward.shape, bf16),
            pltpu.VMEM(inverse.shape, bf16),
            pltpu.VMEM((blocks, chunks, span, LANES), bf16),
            pltpu.VMEM((chunks, blocks, span, LANES), bf16),
            pltpu.VMEM((chunks, blocks, span, LANES), bf16),
            pltpu.VMEM((chunks, blocks, span, LANES), bf16),
            pltpu.VMEM((order, length), f32),
            pltpu.VMEM((blocks, span, own), bf16),
            pltpu.VMEM((blocks + 1, 2, span, own), bf16),
            pltpu.VMEM((blocks + 1, 2 * span, own), f32),
            pltpu.VMEM((blocks + 1, 2, span, LANES), bf16),
            pltpu.VMEM((blocks + 1, 2 * span, LANES), f32),
            pltpu.SemaphoreType.DMA((2,)),
            pltpu.SemaphoreType.DMA((2, chunks, blocks)),
            pltpu.SemaphoreType.DMA((2, chunks, blocks)),
        ],
        compiler_params=pltpu.CompilerParams(
            collective_id=0, has_side_effects=True, vmem_limit_bytes=40 * MIB
        ),
        name="hyena_layer",
    )(
        signal,
        gate_in,
        gate_out,
        jnp.asarray(features),
        pos_weight,
        pos_bias.reshape(1, -1),
        inner_weight,
        inner_bias,
        frequency.reshape(1, -1),
        out_weight,
        decay_rates.reshape(1, -1),
        skip_gain.reshape(1, -1),
        jnp.asarray(forward),
        jnp.asarray(inverse),
    )


def unit_angle(index, period):
    return (index % period).astype(jnp.float32) * (TWO_PI / period)


def section_tables(row_ids, col_ids, period):
    angle = unit_angle(row_ids[:, None] * col_ids[None, :], period)
    return (jnp.cos(angle).astype(jnp.bfloat16), jnp.sin(angle).astype(jnp.bfloat16))


def filter_hidden(positions, total, pos_weight, pos_bias, inner_weight, inner_bias, frequency):
    band_count = (pos_weight.shape[0] - 1) // 2
    position_f = positions.astype(jnp.float32)
    moments = position_f / (total - 1)
    phases = position_f * (TWO_PI / total)
    tone_list = jnp.linspace(0.0001, band_count - 1, band_count).astype(jnp.float32)
    angles = tone_list[:, None] * phases[None, :]
    features = jnp.concatenate([moments[None, :], jnp.cos(angles), -jnp.sin(angles)], axis=0)
    hidden = jnp.sin(
        frequency[:, None]
        * (jnp.dot(pos_weight.T, features, precision=HIGHEST) + pos_bias[:, None])
    )
    for layer_index in range(inner_weight.shape[0]):
        hidden = jnp.sin(
            frequency[:, None]
            * (
                jnp.dot(inner_weight[layer_index].T, hidden, precision=HIGHEST)
                + inner_bias[layer_index][:, None]
            )
        )
    return (hidden, moments)


def plain(
    signal,
    gate_in,
    gate_out,
    pos_weight,
    pos_bias,
    inner_weight,
    inner_bias,
    frequency,
    out_weight,
    decay_rates,
    skip_gain,
):
    blocks = lax.axis_size("seq")
    block_id = lax.axis_index("seq")
    span = signal.shape[1]
    width = signal.shape[2]
    rows_freq = 2 * blocks
    length = span * blocks
    period = 2 * length
    gated = (gate_in[0].astype(jnp.float32) * signal[0].astype(jnp.float32)).astype(jnp.bfloat16)
    fwd_cos, fwd_sin = section_tables(
        jnp.arange(rows_freq, dtype=jnp.int32), jnp.arange(blocks, dtype=jnp.int32), rows_freq
    )
    back_cos, back_sin = section_tables(
        jnp.arange(blocks, dtype=jnp.int32), jnp.arange(rows_freq, dtype=jnp.int32), rows_freq
    )
    column_ids = jnp.arange(span, dtype=jnp.int32)
    own = width // blocks
    lanes = lax.all_to_all(gated.T, "seq", split_axis=0, concat_axis=1, tiled=True)
    own_weight = lax.dynamic_slice_in_dim(out_weight, block_id * own, own, 1)
    own_decay = lax.dynamic_slice_in_dim(decay_rates, block_id * own, own, 0)
    hidden, moments = filter_hidden(
        jnp.arange(length, dtype=jnp.int32),
        length,
        pos_weight,
        pos_bias,
        inner_weight,
        inner_bias,
        frequency,
    )
    shaped = jnp.dot(own_weight.T, hidden, precision=HIGHEST) * (
        jnp.exp(-own_decay[:, None] * moments[None, :]) + FLOOR_SHIFT
    )
    own_scale = lax.rsqrt(jnp.sum(shaped * shaped, axis=1) + EPSILON)
    own_taps = shaped.astype(jnp.bfloat16)

    def first_local(source):
        cube = source.reshape(own, blocks, span)
        real_part = jnp.einsum(
            "ca,oab->cob", fwd_cos, cube, preferred_element_type=jnp.float32
        ).astype(jnp.bfloat16)
        imag_part = (
            -jnp.einsum("ca,oab->cob", fwd_sin, cube, preferred_element_type=jnp.float32)
        ).astype(jnp.bfloat16)
        return (real_part, imag_part)

    data_real, data_imag = first_local(lanes)
    taps_real, taps_imag = first_local(own_taps)
    group = 16
    turns = rows_freq // group

    def grouped(array):
        return array.reshape(turns, group, own, span)

    def row_group(pieces):
        row_real, row_imag, tap_real, tap_imag, row_ids = pieces
        wave_ids = row_ids[:, None] + rows_freq * column_ids[None, :]
        angle = unit_angle(wave_ids[:, :, None] * column_ids[None, None, :], period)
        cosines = jnp.cos(angle).astype(jnp.bfloat16)
        sines = jnp.sin(angle).astype(jnp.bfloat16)

        def spectrum_of(part_real, part_imag):
            spec_real = jnp.einsum(
                "rdb,rob->rod", cosines, part_real, preferred_element_type=jnp.float32
            ) + jnp.einsum("rdb,rob->rod", sines, part_imag, preferred_element_type=jnp.float32)
            spec_imag = jnp.einsum(
                "rdb,rob->rod", cosines, part_imag, preferred_element_type=jnp.float32
            ) - jnp.einsum("rdb,rob->rod", sines, part_real, preferred_element_type=jnp.float32)
            return (spec_real, spec_imag)

        wave_real, wave_imag = spectrum_of(row_real, row_imag)
        spec_real, spec_imag = spectrum_of(tap_real, tap_imag)
        filt_real = spec_real.astype(jnp.bfloat16).astype(jnp.float32)
        filt_imag = spec_imag.astype(jnp.bfloat16).astype(jnp.float32)
        lane_scale = own_scale[None, :, None]
        prod_real = ((wave_real * filt_real - wave_imag * filt_imag) * lane_scale).astype(
            jnp.bfloat16
        )
        prod_imag = ((wave_real * filt_imag + wave_imag * filt_real) * lane_scale).astype(
            jnp.bfloat16
        )
        back_real = jnp.einsum(
            "rdb,rod->rob", cosines, prod_real, preferred_element_type=jnp.float32
        ) - jnp.einsum("rdb,rod->rob", sines, prod_imag, preferred_element_type=jnp.float32)
        back_imag = jnp.einsum(
            "rdb,rod->rob", cosines, prod_imag, preferred_element_type=jnp.float32
        ) + jnp.einsum("rdb,rod->rob", sines, prod_real, preferred_element_type=jnp.float32)
        return (back_real.astype(jnp.bfloat16), back_imag.astype(jnp.bfloat16))

    row_list = jnp.arange(rows_freq, dtype=jnp.int32).reshape(turns, group)
    back_real, back_imag = lax.map(
        row_group,
        (grouped(data_real), grouped(data_imag), grouped(taps_real), grouped(taps_imag), row_list),
    )
    back_real = back_real.reshape(rows_freq, own, span)
    back_imag = back_imag.reshape(rows_freq, own, span)
    local_conv = (
        jnp.einsum("ac,cob->oab", back_cos, back_real, preferred_element_type=jnp.float32)
        - jnp.einsum("ac,cob->oab", back_sin, back_imag, preferred_element_type=jnp.float32)
    ) * (1.0 / period)
    returned = lax.all_to_all(
        local_conv.reshape(own, length).astype(jnp.bfloat16),
        "seq",
        split_axis=1,
        concat_axis=0,
        tiled=True,
    ).astype(jnp.float32)
    convolved_rows = returned.T
    mixed = gate_out[0].astype(jnp.float32) * (
        convolved_rows + skip_gain[None, :] * gated.astype(jnp.float32)
    )
    return mixed.astype(jnp.bfloat16)[None]


def fits_kernel(blocks, span, width):
    own = width // blocks
    power = blocks >= 4 and blocks & (blocks - 1) == 0
    return power and span == LANES and own > 0 and own % LANES == 0


def per_device(signal, *rest):
    if fits_kernel(lax.axis_size("seq"), signal.shape[1], signal.shape[2]):
        return fused(signal, *rest)
    return plain(signal, *rest)


def solution(mesh):
    return jax.shard_map(
        per_device,
        mesh=mesh,
        in_specs=(
            P("grp", "seq", None),
            P("grp", "seq", None),
            P("grp", "seq", None),
            P(),
            P(),
            P(),
            P(),
            P(),
            P(),
            P(),
            P(),
        ),
        out_specs=P("grp", "seq", None),
        check_vma=False,
    )
```

```python
import functools
import math

import jax
import jax.numpy as jnp
import ml_dtypes
import numpy as np
from jax import lax
from jax.experimental import pallas as pl
from jax.experimental.pallas import tpu as pltpu
from jax.sharding import PartitionSpec as P

TWO_PI = 6.283185307179586
FLOOR_SHIFT = 0.05
EPSILON = 1e-06
HIGHEST = lax.Precision.HIGHEST
LANES = 128
MIB = 1024 * 1024


def row_matrices(blocks, span):
    rows_freq = 2 * blocks
    period = rows_freq * span
    ids = np.arange(span, dtype=np.int64)
    wave = np.arange(blocks + 1)[:, None] + rows_freq * ids[None, :]
    turns = (wave[:, :, None] * ids[None, None, :]) % period
    angle = turns.astype(np.float32) * np.float32(TWO_PI / period)
    cosines, sines = np.cos(angle), np.sin(angle)
    upper = np.concatenate([cosines, sines], axis=2)
    lower = np.concatenate([-sines, cosines], axis=2)
    forward = np.concatenate([upper, lower], axis=1).astype(ml_dtypes.bfloat16)
    return forward, np.ascontiguousarray(forward.transpose(0, 2, 1))


def position_features(length, emb):
    band_count = (emb - 1) // 2
    position_f = np.arange(length, dtype=np.float32)
    moments = position_f / np.float32(length - 1)
    phases = position_f * np.float32(TWO_PI / length)
    tones = np.linspace(0.0001, band_count - 1, band_count).astype(np.float32)
    angles = tones[:, None] * phases[None, :]
    return np.concatenate([moments[None, :], np.cos(angles), -np.sin(angles)], axis=0)


def sine(value):
    turns = jnp.round(value * (1.0 / math.pi))
    rest = value - turns * 3.140625
    rest = rest - turns * 9.67502593994140625e-4
    rest = rest - turns * 1.509957990978376432e-7
    parity = turns - 2.0 * jnp.floor(turns * 0.5)
    square = rest * rest
    poly = -2.3889859e-08 * square + 2.7525562e-06
    poly = poly * square - 0.00019840874
    poly = poly * square + 0.0083333310
    poly = poly * square - 0.16666667
    signed = rest - 2.0 * parity * rest
    return signed + signed * (square * poly)


def weighted(terms):
    total = None
    for factor, value in terms:
        if abs(factor) < 1e-9:
            continue
        if abs(factor - 1.0) < 1e-9:
            total = value if total is None else total + value
        elif abs(factor + 1.0) < 1e-9:
            total = -value if total is None else total - value
        else:
            part = value * factor
            total = part if total is None else total + part
    return total


def sections(load, store, blocks):
    half = blocks // 2
    x = [load(a).astype(jnp.float32) for a in range(blocks)]
    plus = {a: x[a] + x[blocks - a] for a in range(1, half)}
    minus = {a: x[a] - x[blocks - a] for a in range(1, half)}
    for c in range(blocks + 1):
        step = math.pi * c / blocks
        even = c % 2 == 0
        on_cos, on_sin = (plus, minus) if even else (minus, plus)
        middle = [(math.cos(step * half), x[half])] if even else []
        real = weighted([(1.0, x[0])] + middle + [(math.cos(step * a), on_cos[a]) for a in on_cos])
        store(c, 0, real.astype(jnp.bfloat16))
        if 0 < c < blocks:
            middle = [] if even else [(-math.sin(step * half), x[half])]
            imag = weighted(middle + [(-math.sin(step * a), on_sin[a]) for a in on_sin])
            store(c, 1, imag.astype(jnp.bfloat16))


def joined(load, store, blocks, factor):
    half = blocks // 2
    real = [load(c, 0) * (factor if c in (0, blocks) else 2.0 * factor) for c in range(blocks + 1)]
    imag = {c: load(c, 1) * (2.0 * factor) for c in range(1, blocks)}
    for a in range(half + 1):
        step = math.pi * a / blocks
        even_cos = weighted([(math.cos(step * c), real[c]) for c in range(0, blocks + 1, 2)])
        odd_cos = weighted([(math.cos(step * c), real[c]) for c in range(1, blocks + 1, 2)])
        even_sin = weighted([(math.sin(step * c), imag[c]) for c in range(2, blocks, 2)])
        odd_sin = weighted([(math.sin(step * c), imag[c]) for c in range(1, blocks, 2)])
        both = even_cos if odd_sin is None else even_cos - odd_sin
        turn = None
        if odd_cos is not None and even_sin is not None:
            turn = odd_cos - even_sin
        elif odd_cos is not None:
            turn = odd_cos
        elif even_sin is not None:
            turn = -even_sin
        store(a, (both if turn is None else both + turn).astype(jnp.bfloat16))
        if 0 < a < half:
            store(blocks - a, (both if turn is None else both - turn).astype(jnp.bfloat16))


def partner(me, mask, count):
    total, bit = 0, 1
    while bit < count:
        digit = (me // bit) % 2
        total = total + bit * ((1 - digit) if mask & bit else digit)
        bit *= 2
    return total


def layer_kernel(
    blocks,
    span,
    own,
    signal_hbm,
    gate_in_hbm,
    gate_out_hbm,
    features_hbm,
    pos_weight_hbm,
    pos_bias_hbm,
    inner_weight_hbm,
    inner_bias_hbm,
    frequency_hbm,
    out_weight_hbm,
    decay_rates_hbm,
    skip_gain_hbm,
    forward_hbm,
    inverse_hbm,
    out,
    signal,
    gate_in,
    gate_out,
    features,
    pos_weight,
    pos_bias,
    inner_weight,
    inner_bias,
    frequency,
    weight,
    decay,
    skip_gain,
    forward,
    inverse,
    gated,
    inbox,
    outbox,
    returned,
    hidden,
    taps,
    tap_rows,
    filt,
    data_rows,
    back,
    load_sem,
    send_sem,
    recv_sem,
):
    me = lax.axis_index("seq")
    chunks = own // LANES
    length = blocks * span
    masks = list(range(blocks - 1, 0, -1))
    peers = {mask: partner(me, mask, blocks) for mask in masks}

    barrier = pltpu.get_barrier_semaphore()
    for mask in masks:
        pl.semaphore_signal(
            barrier, inc=1, device_id={"seq": peers[mask]}, device_id_type=pl.DeviceIdType.MESH
        )
    mine = pl.ds(pl.multiple_of(me * own, LANES), own)
    pairs = [
        (signal_hbm, signal),
        (gate_in_hbm, gate_in),
        (features_hbm, features),
        (pos_weight_hbm, pos_weight),
        (pos_bias_hbm, pos_bias),
        (frequency_hbm, frequency),
        (inner_weight_hbm, inner_weight),
        (inner_bias_hbm, inner_bias),
        (out_weight_hbm.at[:, mine], weight),
        (decay_rates_hbm.at[:, mine], decay),
        (forward_hbm, forward),
        (inverse_hbm, inverse),
        (gate_out_hbm, gate_out),
        (skip_gain_hbm, skip_gain),
    ]
    loads = [
        pltpu.make_async_copy(source, target, load_sem.at[index])
        for index, (source, target) in enumerate(pairs)
    ]
    for copy in loads:
        copy.start()

    for copy in loads[:2]:
        copy.wait()
    for chunk in range(chunks):
        for owner in range(blocks):
            columns = pl.ds(owner * own + chunk * LANES, LANES)
            gated[owner, chunk] = (
                gate_in[0, :, columns].astype(jnp.float32)
                * signal[0, :, columns].astype(jnp.float32)
            ).astype(jnp.bfloat16)
    pl.semaphore_wait(barrier, len(masks))

    def exchange(phase, chunk, source_of, target):
        copies = []
        for mask in masks:
            copy = pltpu.make_async_remote_copy(
                src_ref=source_of(peers[mask]),
                dst_ref=target.at[chunk, me],
                send_sem=send_sem.at[phase, chunk, mask],
                recv_sem=recv_sem.at[phase, chunk, mask],
                device_id={"seq": peers[mask]},
                device_id_type=pl.DeviceIdType.MESH,
            )
            copy.start()
            copies.append(copy)
        return copies

    incoming = [
        exchange(0, chunk, lambda peer, chunk=chunk: gated.at[peer, chunk], inbox)
        for chunk in range(chunks)
    ]
    for chunk in range(chunks):
        inbox[chunk, me] = gated[me, chunk]

    order = frequency.shape[1]
    diagonal = lax.broadcasted_iota(jnp.int32, (order, order), 0) == lax.broadcasted_iota(
        jnp.int32, (order, order), 1
    )

    def as_column(row):
        return jnp.sum(jnp.where(diagonal, row, 0.0), axis=1, keepdims=True)

    def layer(weight, values, bias):
        product = lax.dot_general(
            weight,
            values,
            (((0,), (0,)), ((), ())),
            precision=HIGHEST,
            preferred_element_type=jnp.float32,
        )
        return sine(rate * (product + as_column(bias)))

    for copy in loads[2:10]:
        copy.wait()
    rate = as_column(frequency[...])
    hidden[...] = layer(pos_weight[...], features[...], pos_bias[...])
    for index in range(inner_weight.shape[0]):
        hidden[...] = layer(inner_weight[index], hidden[...], inner_bias[pl.ds(index, 1), :])
    energy = jnp.zeros((1, own), jnp.float32)
    for a in range(blocks):
        place = lax.broadcasted_iota(jnp.int32, (span, own), 0) + a * span
        moment = place.astype(jnp.float32) / float(length - 1)
        raw = lax.dot_general(
            hidden[:, a * span : (a + 1) * span],
            weight[...],
            (((0,), (0,)), ((), ())),
            precision=HIGHEST,
            preferred_element_type=jnp.float32,
        ) * (jnp.exp(-moment * decay[...]) + FLOOR_SHIFT)
        energy = energy + jnp.sum(raw * raw, axis=0, keepdims=True)
        taps[a] = raw.astype(jnp.bfloat16)
    scale = lax.rsqrt(energy + EPSILON)

    group = 16

    def tap_section(step, carry):
        rows = pl.ds(pl.multiple_of(step * group, group), group)

        def store(c, part, value):
            tap_rows[c, part, rows, :] = value

        sections(lambda a: taps[a, rows, :], store, blocks)
        return carry

    lax.fori_loop(0, span // group, tap_section, 0)
    for copy in loads[10:12]:
        copy.wait()

    def spectrum(c, rows):
        if c in (0, blocks):
            table, data = forward[c, :, :span], rows[0]
        else:
            table, data = forward[c], jnp.concatenate([rows[0], rows[1]], axis=0)
        return jnp.dot(table, data, preferred_element_type=jnp.float32)

    for c in range(blocks + 1):
        filt[c] = spectrum(c, tap_rows.at[c]) * scale

    outgoing = []
    for chunk in range(chunks):
        for copy in incoming[chunk]:
            copy.wait_recv()

        def data_section(step, carry):
            rows = pl.ds(pl.multiple_of(step * group, group), group)

            def store(c, part, value):
                data_rows[c, part, rows, :] = value

            sections(lambda a: inbox[chunk, a, rows, :], store, blocks)
            return carry

        lax.fori_loop(0, span // group, data_section, 0)
        lanes = slice(chunk * LANES, (chunk + 1) * LANES)
        for c in range(blocks + 1):
            wave = spectrum(c, data_rows.at[c])
            wave_real, wave_imag = wave[:span], wave[span:]
            filt_real, filt_imag = filt[c, :span, lanes], filt[c, span:, lanes]
            product = jnp.concatenate(
                [
                    (wave_real * filt_real - wave_imag * filt_imag).astype(jnp.bfloat16),
                    (wave_real * filt_imag + wave_imag * filt_real).astype(jnp.bfloat16),
                ],
                axis=0,
            )
            if c in (0, blocks):
                back[c, :span] = jnp.dot(
                    inverse[c, :span, :], product, preferred_element_type=jnp.float32
                )
            else:
                back[c] = jnp.dot(inverse[c], product, preferred_element_type=jnp.float32)

        def join_section(step, carry):
            small = 8

            def load(c, part):
                return back[c, pl.ds(pl.multiple_of(part * span + step * group, small), group), :]

            def store(a, value):
                outbox[chunk, a, pl.ds(pl.multiple_of(step * group, group), group), :] = value

            joined(load, store, blocks, 1.0 / (2 * length))
            return carry

        lax.fori_loop(0, span // group, join_section, 0)
        outgoing.append(
            exchange(1, chunk, lambda peer, chunk=chunk: outbox.at[chunk, peer], returned)
        )

    def finish(chunk, owner, convolved):
        columns = pl.ds(pl.multiple_of(owner * own + chunk * LANES, LANES), LANES)
        out[0, :, columns] = (
            gate_out[0, :, columns].astype(jnp.float32)
            * (
                convolved.astype(jnp.float32)
                + skip_gain[:, columns] * gated[owner, chunk].astype(jnp.float32)
            )
        ).astype(jnp.bfloat16)

    for copy in loads[12:]:
        copy.wait()
    for chunk in range(chunks):
        finish(chunk, me, outbox[chunk, me])
    for chunk in range(chunks):
        for mask, copy in reversed(list(zip(masks, outgoing[chunk]))):
            copy.wait_recv()
            finish(chunk, peers[mask], returned[chunk, peers[mask]])
    for copies in incoming + outgoing:
        for copy in copies:
            copy.wait_send()


def fused(
    signal,
    gate_in,
    gate_out,
    pos_weight,
    pos_bias,
    inner_weight,
    inner_bias,
    frequency,
    out_weight,
    decay_rates,
    skip_gain,
):
    blocks = lax.axis_size("seq")
    span, width = signal.shape[1], signal.shape[2]
    own = width // blocks
    chunks = own // LANES
    length = span * blocks
    order = frequency.shape[0]
    forward, inverse = row_matrices(blocks, span)
    features = position_features(length, pos_weight.shape[0])
    hbm = pl.BlockSpec(memory_space=pltpu.HBM)
    bf16, f32 = jnp.bfloat16, jnp.float32
    operands = (
        signal,
        gate_in,
        gate_out,
        jnp.asarray(features),
        pos_weight,
        pos_bias.reshape(1, -1),
        inner_weight,
        inner_bias,
        frequency.reshape(1, -1),
        out_weight,
        decay_rates.reshape(1, -1),
        skip_gain.reshape(1, -1),
        jnp.asarray(forward),
        jnp.asarray(inverse),
    )
    shapes = [operand.shape for operand in operands]
    shapes[9], shapes[10] = (order, own), (1, own)
    locals_ = [pltpu.VMEM(shape, operand.dtype) for shape, operand in zip(shapes, operands)]
    return pl.pallas_call(
        functools.partial(layer_kernel, blocks, span, own),
        out_shape=jax.ShapeDtypeStruct(signal.shape, bf16),
        in_specs=[hbm] * len(operands),
        out_specs=pl.BlockSpec(memory_space=pltpu.VMEM),
        scratch_shapes=[
            *locals_,
            pltpu.VMEM((blocks, chunks, span, LANES), bf16),
            pltpu.VMEM((chunks, blocks, span, LANES), bf16),
            pltpu.VMEM((chunks, blocks, span, LANES), bf16),
            pltpu.VMEM((chunks, blocks, span, LANES), bf16),
            pltpu.VMEM((order, length), f32),
            pltpu.VMEM((blocks, span, own), bf16),
            pltpu.VMEM((blocks + 1, 2, span, own), bf16),
            pltpu.VMEM((blocks + 1, 2 * span, own), f32),
            pltpu.VMEM((blocks + 1, 2, span, LANES), bf16),
            pltpu.VMEM((blocks + 1, 2 * span, LANES), f32),
            pltpu.SemaphoreType.DMA((len(operands),)),
            pltpu.SemaphoreType.DMA((2, chunks, blocks)),
            pltpu.SemaphoreType.DMA((2, chunks, blocks)),
        ],
        compiler_params=pltpu.CompilerParams(
            collective_id=0, has_side_effects=True, vmem_limit_bytes=62 * MIB
        ),
        name="hyena_layer",
    )(*operands)


def unit_angle(index, period):
    return (index % period).astype(jnp.float32) * (TWO_PI / period)


def section_tables(row_ids, col_ids, period):
    angle = unit_angle(row_ids[:, None] * col_ids[None, :], period)
    return (jnp.cos(angle).astype(jnp.bfloat16), jnp.sin(angle).astype(jnp.bfloat16))


def filter_hidden(positions, total, pos_weight, pos_bias, inner_weight, inner_bias, frequency):
    band_count = (pos_weight.shape[0] - 1) // 2
    position_f = positions.astype(jnp.float32)
    moments = position_f / (total - 1)
    phases = position_f * (TWO_PI / total)
    tone_list = jnp.linspace(0.0001, band_count - 1, band_count).astype(jnp.float32)
    angles = tone_list[:, None] * phases[None, :]
    features = jnp.concatenate([moments[None, :], jnp.cos(angles), -jnp.sin(angles)], axis=0)
    hidden = jnp.sin(
        frequency[:, None]
        * (jnp.dot(pos_weight.T, features, precision=HIGHEST) + pos_bias[:, None])
    )
    for layer_index in range(inner_weight.shape[0]):
        hidden = jnp.sin(
            frequency[:, None]
            * (
                jnp.dot(inner_weight[layer_index].T, hidden, precision=HIGHEST)
                + inner_bias[layer_index][:, None]
            )
        )
    return (hidden, moments)


def plain(
    signal,
    gate_in,
    gate_out,
    pos_weight,
    pos_bias,
    inner_weight,
    inner_bias,
    frequency,
    out_weight,
    decay_rates,
    skip_gain,
):
    blocks = lax.axis_size("seq")
    block_id = lax.axis_index("seq")
    span = signal.shape[1]
    width = signal.shape[2]
    rows_freq = 2 * blocks
    length = span * blocks
    period = 2 * length
    gated = (gate_in[0].astype(jnp.float32) * signal[0].astype(jnp.float32)).astype(jnp.bfloat16)
    fwd_cos, fwd_sin = section_tables(
        jnp.arange(rows_freq, dtype=jnp.int32), jnp.arange(blocks, dtype=jnp.int32), rows_freq
    )
    back_cos, back_sin = section_tables(
        jnp.arange(blocks, dtype=jnp.int32), jnp.arange(rows_freq, dtype=jnp.int32), rows_freq
    )
    column_ids = jnp.arange(span, dtype=jnp.int32)
    own = width // blocks
    lanes = lax.all_to_all(gated.T, "seq", split_axis=0, concat_axis=1, tiled=True)
    own_weight = lax.dynamic_slice_in_dim(out_weight, block_id * own, own, 1)
    own_decay = lax.dynamic_slice_in_dim(decay_rates, block_id * own, own, 0)
    hidden, moments = filter_hidden(
        jnp.arange(length, dtype=jnp.int32),
        length,
        pos_weight,
        pos_bias,
        inner_weight,
        inner_bias,
        frequency,
    )
    shaped = jnp.dot(own_weight.T, hidden, precision=HIGHEST) * (
        jnp.exp(-own_decay[:, None] * moments[None, :]) + FLOOR_SHIFT
    )
    own_scale = lax.rsqrt(jnp.sum(shaped * shaped, axis=1) + EPSILON)
    own_taps = shaped.astype(jnp.bfloat16)

    def first_local(source):
        cube = source.reshape(own, blocks, span)
        real_part = jnp.einsum(
            "ca,oab->cob", fwd_cos, cube, preferred_element_type=jnp.float32
        ).astype(jnp.bfloat16)
        imag_part = (
            -jnp.einsum("ca,oab->cob", fwd_sin, cube, preferred_element_type=jnp.float32)
        ).astype(jnp.bfloat16)
        return (real_part, imag_part)

    data_real, data_imag = first_local(lanes)
    taps_real, taps_imag = first_local(own_taps)
    group = 16
    turns = rows_freq // group

    def grouped(array):
        return array.reshape(turns, group, own, span)

    def row_group(pieces):
        row_real, row_imag, tap_real, tap_imag, row_ids = pieces
        wave_ids = row_ids[:, None] + rows_freq * column_ids[None, :]
        angle = unit_angle(wave_ids[:, :, None] * column_ids[None, None, :], period)
        cosines = jnp.cos(angle).astype(jnp.bfloat16)
        sines = jnp.sin(angle).astype(jnp.bfloat16)

        def spectrum_of(part_real, part_imag):
            spec_real = jnp.einsum(
                "rdb,rob->rod", cosines, part_real, preferred_element_type=jnp.float32
            ) + jnp.einsum("rdb,rob->rod", sines, part_imag, preferred_element_type=jnp.float32)
            spec_imag = jnp.einsum(
                "rdb,rob->rod", cosines, part_imag, preferred_element_type=jnp.float32
            ) - jnp.einsum("rdb,rob->rod", sines, part_real, preferred_element_type=jnp.float32)
            return (spec_real, spec_imag)

        wave_real, wave_imag = spectrum_of(row_real, row_imag)
        spec_real, spec_imag = spectrum_of(tap_real, tap_imag)
        filt_real = spec_real.astype(jnp.bfloat16).astype(jnp.float32)
        filt_imag = spec_imag.astype(jnp.bfloat16).astype(jnp.float32)
        lane_scale = own_scale[None, :, None]
        prod_real = ((wave_real * filt_real - wave_imag * filt_imag) * lane_scale).astype(
            jnp.bfloat16
        )
        prod_imag = ((wave_real * filt_imag + wave_imag * filt_real) * lane_scale).astype(
            jnp.bfloat16
        )
        back_real = jnp.einsum(
            "rdb,rod->rob", cosines, prod_real, preferred_element_type=jnp.float32
        ) - jnp.einsum("rdb,rod->rob", sines, prod_imag, preferred_element_type=jnp.float32)
        back_imag = jnp.einsum(
            "rdb,rod->rob", cosines, prod_imag, preferred_element_type=jnp.float32
        ) + jnp.einsum("rdb,rod->rob", sines, prod_real, preferred_element_type=jnp.float32)
        return (back_real.astype(jnp.bfloat16), back_imag.astype(jnp.bfloat16))

    row_list = jnp.arange(rows_freq, dtype=jnp.int32).reshape(turns, group)
    back_real, back_imag = lax.map(
        row_group,
        (grouped(data_real), grouped(data_imag), grouped(taps_real), grouped(taps_imag), row_list),
    )
    back_real = back_real.reshape(rows_freq, own, span)
    back_imag = back_imag.reshape(rows_freq, own, span)
    local_conv = (
        jnp.einsum("ac,cob->oab", back_cos, back_real, preferred_element_type=jnp.float32)
        - jnp.einsum("ac,cob->oab", back_sin, back_imag, preferred_element_type=jnp.float32)
    ) * (1.0 / period)
    returned = lax.all_to_all(
        local_conv.reshape(own, length).astype(jnp.bfloat16),
        "seq",
        split_axis=1,
        concat_axis=0,
        tiled=True,
    ).astype(jnp.float32)
    convolved_rows = returned.T
    mixed = gate_out[0].astype(jnp.float32) * (
        convolved_rows + skip_gain[None, :] * gated.astype(jnp.float32)
    )
    return mixed.astype(jnp.bfloat16)[None]


def fits_kernel(blocks, span, width):
    own = width // blocks
    power = blocks >= 4 and blocks & (blocks - 1) == 0
    return power and span == LANES and own > 0 and own % LANES == 0


def per_device(signal, *rest):
    if fits_kernel(lax.axis_size("seq"), signal.shape[1], signal.shape[2]):
        return fused(signal, *rest)
    return plain(signal, *rest)


def solution(mesh):
    return jax.shard_map(
        per_device,
        mesh=mesh,
        in_specs=(
            P("grp", "seq", None),
            P("grp", "seq", None),
            P("grp", "seq", None),
            P(),
            P(),
            P(),
            P(),
            P(),
            P(),
            P(),
            P(),
        ),
        out_specs=P("grp", "seq", None),
        check_vma=False,
    )
```

```python
import functools
import math

import jax
import jax.numpy as jnp
import ml_dtypes
import numpy as np
from jax import lax
from jax.experimental import pallas as pl
from jax.experimental.pallas import tpu as pltpu
from jax.sharding import PartitionSpec as P

TWO_PI = 6.283185307179586
FLOOR_SHIFT = 0.05
EPSILON = 1e-06
HIGHEST = lax.Precision.HIGHEST
LANES = 128
MIB = 1024 * 1024


def row_matrices(blocks, span):
    rows_freq = 2 * blocks
    period = rows_freq * span
    ids = np.arange(span, dtype=np.int64)
    wave = np.arange(blocks + 1)[:, None] + rows_freq * ids[None, :]
    turns = (wave[:, :, None] * ids[None, None, :]) % period
    angle = turns.astype(np.float32) * np.float32(TWO_PI / period)
    cosines, sines = np.cos(angle), np.sin(angle)
    upper = np.concatenate([cosines, sines], axis=2)
    lower = np.concatenate([-sines, cosines], axis=2)
    forward = np.concatenate([upper, lower], axis=1).astype(ml_dtypes.bfloat16)
    return forward, np.ascontiguousarray(forward.transpose(0, 2, 1))


def padded(rows):
    return -(-rows // 8) * 8


def position_features(length, emb):
    band_count = (emb - 1) // 2
    position_f = np.arange(length, dtype=np.float32)
    moments = position_f / np.float32(length - 1)
    phases = position_f * np.float32(TWO_PI / length)
    tones = np.linspace(0.0001, band_count - 1, band_count).astype(np.float32)
    angles = tones[:, None] * phases[None, :]
    features = np.concatenate([moments[None, :], np.cos(angles), -np.sin(angles)], axis=0)
    rest = np.pad(features, ((0, padded(emb) - emb), (0, 0)))
    parts = []
    for _ in range(3):
        parts.append(rest.astype(ml_dtypes.bfloat16).astype(np.float32))
        rest = rest - parts[-1]
    rows = np.concatenate([parts[index] for index in RIGHT_ORDER], axis=0)
    return rows.astype(ml_dtypes.bfloat16)


def sine(value):
    turns = jnp.round(value * (1.0 / math.pi))
    rest = value - turns * 3.140625
    rest = rest - turns * 9.67502593994140625e-4
    rest = rest - turns * 1.509957990978376432e-7
    parity = turns - 2.0 * jnp.floor(turns * 0.5)
    square = rest * rest
    poly = -2.3889859e-08 * square + 2.7525562e-06
    poly = poly * square - 0.00019840874
    poly = poly * square + 0.0083333310
    poly = poly * square - 0.16666667
    signed = rest - 2.0 * parity * rest
    return signed + signed * (square * poly)


def pieces(value, count):
    parts = []
    for _ in range(count):
        part = value.astype(jnp.bfloat16).astype(jnp.float32)
        parts.append(part)
        value = value - part
    return parts


LEFT_ORDER, RIGHT_ORDER = (0, 1, 0, 1, 0, 2), (0, 0, 1, 1, 2, 0)


def stacked(parts, order):
    return jnp.concatenate([parts[index] for index in order], axis=0).astype(jnp.bfloat16)


def stacked_dot(left, right):
    return lax.dot_general(
        left, right, (((0,), (0,)), ((), ())), preferred_element_type=jnp.float32
    )


def weighted(terms):
    total = None
    for factor, value in terms:
        if abs(factor) < 1e-9:
            continue
        if abs(factor - 1.0) < 1e-9:
            total = value if total is None else total + value
        elif abs(factor + 1.0) < 1e-9:
            total = -value if total is None else total - value
        else:
            part = value * factor
            total = part if total is None else total + part
    return total


def sections(load, store, blocks):
    half = blocks // 2
    x = [load(a).astype(jnp.float32) for a in range(blocks)]
    plus = {a: x[a] + x[blocks - a] for a in range(1, half)}
    minus = {a: x[a] - x[blocks - a] for a in range(1, half)}
    for c in range(blocks + 1):
        step = math.pi * c / blocks
        even = c % 2 == 0
        on_cos, on_sin = (plus, minus) if even else (minus, plus)
        middle = [(math.cos(step * half), x[half])] if even else []
        real = weighted([(1.0, x[0])] + middle + [(math.cos(step * a), on_cos[a]) for a in on_cos])
        store(c, 0, real.astype(jnp.bfloat16))
        if 0 < c < blocks:
            middle = [] if even else [(-math.sin(step * half), x[half])]
            imag = weighted(middle + [(-math.sin(step * a), on_sin[a]) for a in on_sin])
            store(c, 1, imag.astype(jnp.bfloat16))


def joined(load, store, blocks, factor):
    half = blocks // 2
    real = [load(c, 0) * (factor if c in (0, blocks) else 2.0 * factor) for c in range(blocks + 1)]
    imag = {c: load(c, 1) * (2.0 * factor) for c in range(1, blocks)}
    for a in range(half + 1):
        step = math.pi * a / blocks
        even_cos = weighted([(math.cos(step * c), real[c]) for c in range(0, blocks + 1, 2)])
        odd_cos = weighted([(math.cos(step * c), real[c]) for c in range(1, blocks + 1, 2)])
        even_sin = weighted([(math.sin(step * c), imag[c]) for c in range(2, blocks, 2)])
        odd_sin = weighted([(math.sin(step * c), imag[c]) for c in range(1, blocks, 2)])
        both = even_cos if odd_sin is None else even_cos - odd_sin
        turn = None
        if odd_cos is not None and even_sin is not None:
            turn = odd_cos - even_sin
        elif odd_cos is not None:
            turn = odd_cos
        elif even_sin is not None:
            turn = -even_sin
        store(a, (both if turn is None else both + turn).astype(jnp.bfloat16))
        if 0 < a < half:
            store(blocks - a, (both if turn is None else both - turn).astype(jnp.bfloat16))


def partner(me, mask, count):
    total, bit = 0, 1
    while bit < count:
        digit = (me // bit) % 2
        total = total + bit * ((1 - digit) if mask & bit else digit)
        bit *= 2
    return total


def layer_kernel(
    blocks,
    span,
    own,
    signal_hbm,
    gate_in_hbm,
    gate_out_hbm,
    features_hbm,
    pos_weight_hbm,
    pos_bias_hbm,
    inner_weight_hbm,
    inner_bias_hbm,
    frequency_hbm,
    out_weight_hbm,
    decay_rates_hbm,
    skip_gain_hbm,
    forward_hbm,
    inverse_hbm,
    out,
    signal,
    gate_in,
    gate_out,
    features,
    pos_weight,
    pos_bias,
    inner_weight,
    inner_bias,
    frequency,
    weight,
    decay,
    skip_gain,
    forward,
    inverse,
    staged,
    wide_weight,
    gated,
    inbox,
    outbox,
    returned,
    hidden,
    taps,
    tap_rows,
    filt,
    data_rows,
    back,
    load_sem,
    leave_sem,
    send_sem,
    recv_sem,
):
    me = lax.axis_index("seq")
    chunks = own // LANES
    length = blocks * span
    masks = list(range(blocks - 1, 0, -1))
    peers = {mask: partner(me, mask, blocks) for mask in masks}

    barrier = pltpu.get_barrier_semaphore()
    for mask in masks:
        pl.semaphore_signal(
            barrier, inc=1, device_id={"seq": peers[mask]}, device_id_type=pl.DeviceIdType.MESH
        )
    mine = pl.ds(pl.multiple_of(me * own, LANES), own)
    pairs = [
        (signal_hbm, signal),
        (gate_in_hbm, gate_in),
        (features_hbm, features),
        (pos_weight_hbm, pos_weight),
        (pos_bias_hbm, pos_bias),
        (frequency_hbm, frequency),
        (inner_weight_hbm, inner_weight),
        (inner_bias_hbm, inner_bias),
        (out_weight_hbm.at[:, mine], weight),
        (decay_rates_hbm.at[:, mine], decay),
        (forward_hbm, forward),
        (inverse_hbm, inverse),
        (gate_out_hbm, gate_out),
        (skip_gain_hbm, skip_gain),
    ]
    loads = [
        pltpu.make_async_copy(source, target, load_sem.at[index])
        for index, (source, target) in enumerate(pairs)
    ]
    for copy in loads:
        copy.start()

    for copy in loads[:2]:
        copy.wait()
    for chunk in range(chunks):
        for owner in range(blocks):
            columns = pl.ds(owner * own + chunk * LANES, LANES)
            gated[owner, chunk] = (
                gate_in[0, :, columns].astype(jnp.float32)
                * signal[0, :, columns].astype(jnp.float32)
            ).astype(jnp.bfloat16)
    pl.semaphore_wait(barrier, len(masks))

    def exchange(phase, chunk, source_of, target):
        copies = []
        for mask in masks:
            copy = pltpu.make_async_remote_copy(
                src_ref=source_of(peers[mask]),
                dst_ref=target.at[chunk, me],
                send_sem=send_sem.at[phase, chunk, mask],
                recv_sem=recv_sem.at[phase, chunk, mask],
                device_id={"seq": peers[mask]},
                device_id_type=pl.DeviceIdType.MESH,
            )
            copy.start()
            copies.append(copy)
        return copies

    incoming = [
        exchange(0, chunk, lambda peer, chunk=chunk: gated.at[peer, chunk], inbox)
        for chunk in range(chunks)
    ]
    for chunk in range(chunks):
        inbox[chunk, me] = gated[me, chunk]

    order = frequency.shape[1]
    diagonal = lax.broadcasted_iota(jnp.int32, (order, order), 0) == lax.broadcasted_iota(
        jnp.int32, (order, order), 1
    )

    def as_column(row):
        return jnp.sum(jnp.where(diagonal, row, 0.0), axis=1, keepdims=True)

    def layer(left, right, bias):
        return sine(rate * (stacked_dot(left, right) + as_column(bias)))

    for copy in loads[2:10]:
        copy.wait()
    rate = as_column(frequency[...])
    wide_weight[...] = jnp.zeros_like(wide_weight)
    wide_weight[: pos_weight.shape[0], :] = pos_weight[...]
    left = stacked(pieces(wide_weight[...], 3), LEFT_ORDER)
    hidden[...] = layer(left, features[...], pos_bias[...])
    for index in range(inner_weight.shape[0]):
        left = stacked(pieces(inner_weight[index], 3), LEFT_ORDER)
        right = stacked(pieces(hidden[...], 3), RIGHT_ORDER)
        hidden[...] = layer(left, right, inner_bias[pl.ds(index, 1), :])
    right = stacked(pieces(weight[...], 2), (0, 0, 1, 1))
    energy = jnp.zeros((1, own), jnp.float32)
    for a in range(blocks):
        place = lax.broadcasted_iota(jnp.int32, (span, own), 0) + a * span
        moment = place.astype(jnp.float32) / float(length - 1)
        left = stacked(pieces(hidden[:, a * span : (a + 1) * span], 2), (0, 1, 0, 1))
        raw = stacked_dot(left, right) * (jnp.exp(-moment * decay[...]) + FLOOR_SHIFT)
        energy = energy + jnp.sum(raw * raw, axis=0, keepdims=True)
        taps[a] = raw.astype(jnp.bfloat16)
    scale = lax.rsqrt(energy + EPSILON)

    group = 16

    def tap_section(step, carry):
        rows = pl.ds(pl.multiple_of(step * group, group), group)

        def store(c, part, value):
            tap_rows[c, part, rows, :] = value

        sections(lambda a: taps[a, rows, :], store, blocks)
        return carry

    lax.fori_loop(0, span // group, tap_section, 0)
    for copy in loads[10:12]:
        copy.wait()

    def spectrum(c, rows):
        if c in (0, blocks):
            table, data = forward[c, :, :span], rows[0]
        else:
            table, data = forward[c], jnp.concatenate([rows[0], rows[1]], axis=0)
        return jnp.dot(table, data, preferred_element_type=jnp.float32)

    for c in range(blocks + 1):
        filt[c] = spectrum(c, tap_rows.at[c]) * scale

    outgoing = []
    for chunk in range(chunks):
        for copy in incoming[chunk]:
            copy.wait_recv()

        def data_section(step, carry):
            rows = pl.ds(pl.multiple_of(step * group, group), group)

            def store(c, part, value):
                data_rows[c, part, rows, :] = value

            sections(lambda a: inbox[chunk, a, rows, :], store, blocks)
            return carry

        lax.fori_loop(0, span // group, data_section, 0)
        lanes = slice(chunk * LANES, (chunk + 1) * LANES)
        for c in range(blocks + 1):
            wave = spectrum(c, data_rows.at[c])
            wave_real, wave_imag = wave[:span], wave[span:]
            filt_real, filt_imag = filt[c, :span, lanes], filt[c, span:, lanes]
            product = jnp.concatenate(
                [
                    (wave_real * filt_real - wave_imag * filt_imag).astype(jnp.bfloat16),
                    (wave_real * filt_imag + wave_imag * filt_real).astype(jnp.bfloat16),
                ],
                axis=0,
            )
            if c in (0, blocks):
                back[c, :span] = jnp.dot(
                    inverse[c, :span, :], product, preferred_element_type=jnp.float32
                )
            else:
                back[c] = jnp.dot(inverse[c], product, preferred_element_type=jnp.float32)

        def join_section(step, carry):
            small = 8

            def load(c, part):
                return back[c, pl.ds(pl.multiple_of(part * span + step * group, small), group), :]

            def store(a, value):
                outbox[chunk, a, pl.ds(pl.multiple_of(step * group, group), group), :] = value

            joined(load, store, blocks, 1.0 / (2 * length))
            return carry

        lax.fori_loop(0, span // group, join_section, 0)
        outgoing.append(
            exchange(1, chunk, lambda peer, chunk=chunk: outbox.at[chunk, peer], returned)
        )

    def finish(chunk, slot, owner, convolved):
        columns = pl.ds(pl.multiple_of(owner * own + chunk * LANES, LANES), LANES)
        staged[0, :, columns] = (
            gate_out[0, :, columns].astype(jnp.float32)
            * (
                convolved.astype(jnp.float32)
                + skip_gain[:, columns] * gated[owner, chunk].astype(jnp.float32)
            )
        ).astype(jnp.bfloat16)
        copy = pltpu.make_async_copy(
            staged.at[:, :, columns], out.at[:, :, columns], leave_sem.at[chunk, slot]
        )
        copy.start()
        leaving.append(copy)

    leaving = []
    for copy in loads[12:]:
        copy.wait()
    for chunk in range(chunks):
        finish(chunk, 0, me, outbox[chunk, me])
    for chunk in range(chunks):
        for mask, copy in reversed(list(zip(masks, outgoing[chunk]))):
            copy.wait_recv()
            finish(chunk, mask, peers[mask], returned[chunk, peers[mask]])
    for copy in leaving:
        copy.wait()
    for copies in incoming + outgoing:
        for copy in copies:
            copy.wait_send()


def fused(
    signal,
    gate_in,
    gate_out,
    pos_weight,
    pos_bias,
    inner_weight,
    inner_bias,
    frequency,
    out_weight,
    decay_rates,
    skip_gain,
):
    blocks = lax.axis_size("seq")
    span, width = signal.shape[1], signal.shape[2]
    own = width // blocks
    chunks = own // LANES
    length = span * blocks
    order = frequency.shape[0]
    forward, inverse = row_matrices(blocks, span)
    features = position_features(length, pos_weight.shape[0])
    hbm = pl.BlockSpec(memory_space=pltpu.HBM)
    bf16, f32 = jnp.bfloat16, jnp.float32
    operands = (
        signal,
        gate_in,
        gate_out,
        jnp.asarray(features),
        pos_weight,
        pos_bias.reshape(1, -1),
        inner_weight,
        inner_bias,
        frequency.reshape(1, -1),
        out_weight,
        decay_rates.reshape(1, -1),
        skip_gain.reshape(1, -1),
        jnp.asarray(forward),
        jnp.asarray(inverse),
    )
    shapes = [operand.shape for operand in operands]
    shapes[9], shapes[10] = (order, own), (1, own)
    locals_ = [pltpu.VMEM(shape, operand.dtype) for shape, operand in zip(shapes, operands)]
    return pl.pallas_call(
        functools.partial(layer_kernel, blocks, span, own),
        out_shape=jax.ShapeDtypeStruct(signal.shape, bf16),
        in_specs=[hbm] * len(operands),
        out_specs=hbm,
        scratch_shapes=[
            *locals_,
            pltpu.VMEM(signal.shape, bf16),
            pltpu.VMEM((padded(pos_weight.shape[0]), order), f32),
            pltpu.VMEM((blocks, chunks, span, LANES), bf16),
            pltpu.VMEM((chunks, blocks, span, LANES), bf16),
            pltpu.VMEM((chunks, blocks, span, LANES), bf16),
            pltpu.VMEM((chunks, blocks, span, LANES), bf16),
            pltpu.VMEM((order, length), f32),
            pltpu.VMEM((blocks, span, own), bf16),
            pltpu.VMEM((blocks + 1, 2, span, own), bf16),
            pltpu.VMEM((blocks + 1, 2 * span, own), f32),
            pltpu.VMEM((blocks + 1, 2, span, LANES), bf16),
            pltpu.VMEM((blocks + 1, 2 * span, LANES), f32),
            pltpu.SemaphoreType.DMA((len(operands),)),
            pltpu.SemaphoreType.DMA((chunks, blocks)),
            pltpu.SemaphoreType.DMA((2, chunks, blocks)),
            pltpu.SemaphoreType.DMA((2, chunks, blocks)),
        ],
        compiler_params=pltpu.CompilerParams(
            collective_id=0, has_side_effects=True, vmem_limit_bytes=62 * MIB
        ),
        name="hyena_layer",
    )(*operands)


def unit_angle(index, period):
    return (index % period).astype(jnp.float32) * (TWO_PI / period)


def section_tables(row_ids, col_ids, period):
    angle = unit_angle(row_ids[:, None] * col_ids[None, :], period)
    return (jnp.cos(angle).astype(jnp.bfloat16), jnp.sin(angle).astype(jnp.bfloat16))


def filter_hidden(positions, total, pos_weight, pos_bias, inner_weight, inner_bias, frequency):
    band_count = (pos_weight.shape[0] - 1) // 2
    position_f = positions.astype(jnp.float32)
    moments = position_f / (total - 1)
    phases = position_f * (TWO_PI / total)
    tone_list = jnp.linspace(0.0001, band_count - 1, band_count).astype(jnp.float32)
    angles = tone_list[:, None] * phases[None, :]
    features = jnp.concatenate([moments[None, :], jnp.cos(angles), -jnp.sin(angles)], axis=0)
    hidden = jnp.sin(
        frequency[:, None]
        * (jnp.dot(pos_weight.T, features, precision=HIGHEST) + pos_bias[:, None])
    )
    for layer_index in range(inner_weight.shape[0]):
        hidden = jnp.sin(
            frequency[:, None]
            * (
                jnp.dot(inner_weight[layer_index].T, hidden, precision=HIGHEST)
                + inner_bias[layer_index][:, None]
            )
        )
    return (hidden, moments)


def plain(
    signal,
    gate_in,
    gate_out,
    pos_weight,
    pos_bias,
    inner_weight,
    inner_bias,
    frequency,
    out_weight,
    decay_rates,
    skip_gain,
):
    blocks = lax.axis_size("seq")
    block_id = lax.axis_index("seq")
    span = signal.shape[1]
    width = signal.shape[2]
    rows_freq = 2 * blocks
    length = span * blocks
    period = 2 * length
    gated = (gate_in[0].astype(jnp.float32) * signal[0].astype(jnp.float32)).astype(jnp.bfloat16)
    fwd_cos, fwd_sin = section_tables(
        jnp.arange(rows_freq, dtype=jnp.int32), jnp.arange(blocks, dtype=jnp.int32), rows_freq
    )
    back_cos, back_sin = section_tables(
        jnp.arange(blocks, dtype=jnp.int32), jnp.arange(rows_freq, dtype=jnp.int32), rows_freq
    )
    column_ids = jnp.arange(span, dtype=jnp.int32)
    own = width // blocks
    lanes = lax.all_to_all(gated.T, "seq", split_axis=0, concat_axis=1, tiled=True)
    own_weight = lax.dynamic_slice_in_dim(out_weight, block_id * own, own, 1)
    own_decay = lax.dynamic_slice_in_dim(decay_rates, block_id * own, own, 0)
    hidden, moments = filter_hidden(
        jnp.arange(length, dtype=jnp.int32),
        length,
        pos_weight,
        pos_bias,
        inner_weight,
        inner_bias,
        frequency,
    )
    shaped = jnp.dot(own_weight.T, hidden, precision=HIGHEST) * (
        jnp.exp(-own_decay[:, None] * moments[None, :]) + FLOOR_SHIFT
    )
    own_scale = lax.rsqrt(jnp.sum(shaped * shaped, axis=1) + EPSILON)
    own_taps = shaped.astype(jnp.bfloat16)

    def first_local(source):
        cube = source.reshape(own, blocks, span)
        real_part = jnp.einsum(
            "ca,oab->cob", fwd_cos, cube, preferred_element_type=jnp.float32
        ).astype(jnp.bfloat16)
        imag_part = (
            -jnp.einsum("ca,oab->cob", fwd_sin, cube, preferred_element_type=jnp.float32)
        ).astype(jnp.bfloat16)
        return (real_part, imag_part)

    data_real, data_imag = first_local(lanes)
    taps_real, taps_imag = first_local(own_taps)
    group = 16
    turns = rows_freq // group

    def grouped(array):
        return array.reshape(turns, group, own, span)

    def row_group(pieces):
        row_real, row_imag, tap_real, tap_imag, row_ids = pieces
        wave_ids = row_ids[:, None] + rows_freq * column_ids[None, :]
        angle = unit_angle(wave_ids[:, :, None] * column_ids[None, None, :], period)
        cosines = jnp.cos(angle).astype(jnp.bfloat16)
        sines = jnp.sin(angle).astype(jnp.bfloat16)

        def spectrum_of(part_real, part_imag):
            spec_real = jnp.einsum(
                "rdb,rob->rod", cosines, part_real, preferred_element_type=jnp.float32
            ) + jnp.einsum("rdb,rob->rod", sines, part_imag, preferred_element_type=jnp.float32)
            spec_imag = jnp.einsum(
                "rdb,rob->rod", cosines, part_imag, preferred_element_type=jnp.float32
            ) - jnp.einsum("rdb,rob->rod", sines, part_real, preferred_element_type=jnp.float32)
            return (spec_real, spec_imag)

        wave_real, wave_imag = spectrum_of(row_real, row_imag)
        spec_real, spec_imag = spectrum_of(tap_real, tap_imag)
        filt_real = spec_real.astype(jnp.bfloat16).astype(jnp.float32)
        filt_imag = spec_imag.astype(jnp.bfloat16).astype(jnp.float32)
        lane_scale = own_scale[None, :, None]
        prod_real = ((wave_real * filt_real - wave_imag * filt_imag) * lane_scale).astype(
            jnp.bfloat16
        )
        prod_imag = ((wave_real * filt_imag + wave_imag * filt_real) * lane_scale).astype(
            jnp.bfloat16
        )
        back_real = jnp.einsum(
            "rdb,rod->rob", cosines, prod_real, preferred_element_type=jnp.float32
        ) - jnp.einsum("rdb,rod->rob", sines, prod_imag, preferred_element_type=jnp.float32)
        back_imag = jnp.einsum(
            "rdb,rod->rob", cosines, prod_imag, preferred_element_type=jnp.float32
        ) + jnp.einsum("rdb,rod->rob", sines, prod_real, preferred_element_type=jnp.float32)
        return (back_real.astype(jnp.bfloat16), back_imag.astype(jnp.bfloat16))

    row_list = jnp.arange(rows_freq, dtype=jnp.int32).reshape(turns, group)
    back_real, back_imag = lax.map(
        row_group,
        (grouped(data_real), grouped(data_imag), grouped(taps_real), grouped(taps_imag), row_list),
    )
    back_real = back_real.reshape(rows_freq, own, span)
    back_imag = back_imag.reshape(rows_freq, own, span)
    local_conv = (
        jnp.einsum("ac,cob->oab", back_cos, back_real, preferred_element_type=jnp.float32)
        - jnp.einsum("ac,cob->oab", back_sin, back_imag, preferred_element_type=jnp.float32)
    ) * (1.0 / period)
    returned = lax.all_to_all(
        local_conv.reshape(own, length).astype(jnp.bfloat16),
        "seq",
        split_axis=1,
        concat_axis=0,
        tiled=True,
    ).astype(jnp.float32)
    convolved_rows = returned.T
    mixed = gate_out[0].astype(jnp.float32) * (
        convolved_rows + skip_gain[None, :] * gated.astype(jnp.float32)
    )
    return mixed.astype(jnp.bfloat16)[None]


def fits_kernel(blocks, span, width):
    own = width // blocks
    power = blocks >= 4 and blocks & (blocks - 1) == 0
    return power and span == LANES and own > 0 and own % LANES == 0


def per_device(signal, *rest):
    if fits_kernel(lax.axis_size("seq"), signal.shape[1], signal.shape[2]):
        return fused(signal, *rest)
    return plain(signal, *rest)


def solution(mesh):
    return jax.shard_map(
        per_device,
        mesh=mesh,
        in_specs=(
            P("grp", "seq", None),
            P("grp", "seq", None),
            P("grp", "seq", None),
            P(),
            P(),
            P(),
            P(),
            P(),
            P(),
            P(),
            P(),
        ),
        out_specs=P("grp", "seq", None),
        check_vma=False,
    )
```

```python
import functools
import math

import jax
import jax.numpy as jnp
import ml_dtypes
import numpy as np
from jax import lax
from jax.experimental import pallas as pl
from jax.experimental.pallas import tpu as pltpu
from jax.sharding import PartitionSpec as P

TWO_PI = 6.283185307179586
FLOOR_SHIFT = 0.05
EPSILON = 1e-06
HIGHEST = lax.Precision.HIGHEST
LANES = 128
MIB = 1024 * 1024


def row_matrices(blocks, span):
    rows_freq = 2 * blocks
    period = rows_freq * span
    ids = np.arange(span, dtype=np.int64)
    wave = np.arange(blocks + 1)[:, None] + rows_freq * ids[None, :]
    turns = (wave[:, :, None] * ids[None, None, :]) % period
    angle = turns.astype(np.float32) * np.float32(TWO_PI / period)
    cosines, sines = np.cos(angle), np.sin(angle)
    upper = np.concatenate([cosines, sines], axis=2)
    lower = np.concatenate([-sines, cosines], axis=2)
    forward = np.concatenate([upper, lower], axis=1).astype(ml_dtypes.bfloat16)
    return forward, np.ascontiguousarray(forward.transpose(0, 2, 1))


def padded(rows):
    return -(-rows // 8) * 8


def position_features(length, emb):
    band_count = (emb - 1) // 2
    position_f = np.arange(length, dtype=np.float32)
    moments = position_f / np.float32(length - 1)
    phases = position_f * np.float32(TWO_PI / length)
    tones = np.linspace(0.0001, band_count - 1, band_count).astype(np.float32)
    angles = tones[:, None] * phases[None, :]
    features = np.concatenate([moments[None, :], np.cos(angles), -np.sin(angles)], axis=0)
    rest = np.pad(features, ((0, padded(emb) - emb), (0, 0)))
    parts = []
    for _ in range(3):
        parts.append(rest.astype(ml_dtypes.bfloat16).astype(np.float32))
        rest = rest - parts[-1]
    rows = np.concatenate([parts[index] for index in RIGHT_ORDER], axis=0)
    return rows.astype(ml_dtypes.bfloat16)


def sine(value):
    turns = jnp.round(value * (1.0 / math.pi))
    rest = value - turns * 3.140625
    rest = rest - turns * 9.67502593994140625e-4
    rest = rest - turns * 1.509957990978376432e-7
    parity = turns - 2.0 * jnp.floor(turns * 0.5)
    square = rest * rest
    poly = -2.3889859e-08 * square + 2.7525562e-06
    poly = poly * square - 0.00019840874
    poly = poly * square + 0.0083333310
    poly = poly * square - 0.16666667
    signed = rest - 2.0 * parity * rest
    return signed + signed * (square * poly)


def pieces(value, count):
    parts = []
    for _ in range(count):
        part = value.astype(jnp.bfloat16).astype(jnp.float32)
        parts.append(part)
        value = value - part
    return parts


LEFT_ORDER, RIGHT_ORDER = (0, 1, 0, 1, 0, 2), (0, 0, 1, 1, 2, 0)


def stacked(parts, order):
    return jnp.concatenate([parts[index] for index in order], axis=0).astype(jnp.bfloat16)


def stacked_dot(left, right):
    return lax.dot_general(
        left, right, (((0,), (0,)), ((), ())), preferred_element_type=jnp.float32
    )


def weighted(terms):
    total = None
    for factor, value in terms:
        if abs(factor) < 1e-9:
            continue
        if abs(factor - 1.0) < 1e-9:
            total = value if total is None else total + value
        elif abs(factor + 1.0) < 1e-9:
            total = -value if total is None else total - value
        else:
            part = value * factor
            total = part if total is None else total + part
    return total


def sections(load, store, blocks):
    half = blocks // 2
    x = [load(a).astype(jnp.float32) for a in range(blocks)]
    plus = {a: x[a] + x[blocks - a] for a in range(1, half)}
    minus = {a: x[a] - x[blocks - a] for a in range(1, half)}
    for c in range(blocks + 1):
        step = math.pi * c / blocks
        even = c % 2 == 0
        on_cos, on_sin = (plus, minus) if even else (minus, plus)
        middle = [(math.cos(step * half), x[half])] if even else []
        real = weighted([(1.0, x[0])] + middle + [(math.cos(step * a), on_cos[a]) for a in on_cos])
        store(c, 0, real.astype(jnp.bfloat16))
        if 0 < c < blocks:
            middle = [] if even else [(-math.sin(step * half), x[half])]
            imag = weighted(middle + [(-math.sin(step * a), on_sin[a]) for a in on_sin])
            store(c, 1, imag.astype(jnp.bfloat16))


def joined(load, store, blocks, factor):
    half = blocks // 2
    real = [load(c, 0) * (factor if c in (0, blocks) else 2.0 * factor) for c in range(blocks + 1)]
    imag = {c: load(c, 1) * (2.0 * factor) for c in range(1, blocks)}
    for a in range(half + 1):
        step = math.pi * a / blocks
        even_cos = weighted([(math.cos(step * c), real[c]) for c in range(0, blocks + 1, 2)])
        odd_cos = weighted([(math.cos(step * c), real[c]) for c in range(1, blocks + 1, 2)])
        even_sin = weighted([(math.sin(step * c), imag[c]) for c in range(2, blocks, 2)])
        odd_sin = weighted([(math.sin(step * c), imag[c]) for c in range(1, blocks, 2)])
        both = even_cos if odd_sin is None else even_cos - odd_sin
        turn = None
        if odd_cos is not None and even_sin is not None:
            turn = odd_cos - even_sin
        elif odd_cos is not None:
            turn = odd_cos
        elif even_sin is not None:
            turn = -even_sin
        store(a, (both if turn is None else both + turn).astype(jnp.bfloat16))
        if 0 < a < half:
            store(blocks - a, (both if turn is None else both - turn).astype(jnp.bfloat16))


def partner(me, mask, count):
    total, bit = 0, 1
    while bit < count:
        digit, flip = (me // bit) % 2, (mask // bit) % 2
        total = total + bit * (digit + flip - 2 * digit * flip)
        bit *= 2
    return total


def layer_kernel(
    blocks,
    span,
    own,
    signal_hbm,
    gate_in_hbm,
    gate_out_hbm,
    features_hbm,
    pos_weight_hbm,
    pos_bias_hbm,
    inner_weight_hbm,
    inner_bias_hbm,
    frequency_hbm,
    out_weight_hbm,
    decay_rates_hbm,
    skip_gain_hbm,
    forward_hbm,
    inverse_hbm,
    out,
    signal,
    gate_in,
    gate_out,
    features,
    pos_weight,
    pos_bias,
    inner_weight,
    inner_bias,
    frequency,
    weight,
    decay,
    skip_gain,
    forward,
    inverse,
    staged,
    wide_weight,
    gated,
    inbox,
    outbox,
    returned,
    hidden,
    taps,
    tap_rows,
    filt,
    data_rows,
    back,
    load_sem,
    leave_sem,
    send_sem,
    recv_sem,
):
    me = lax.axis_index("seq")
    chunks = own // LANES
    length = blocks * span
    far_first = list(range(blocks - 1, 0, -1))
    near_first = far_first[blocks // 2 :] + far_first[: blocks // 2]
    odd = lax.axis_index("grp") % 2
    peers = [partner(me, a + (b - a) * odd, blocks) for a, b in zip(far_first, near_first)]

    barrier = pltpu.get_barrier_semaphore()
    for peer in peers:
        pl.semaphore_signal(
            barrier, inc=1, device_id={"seq": peer}, device_id_type=pl.DeviceIdType.MESH
        )
    mine = pl.ds(pl.multiple_of(me * own, LANES), own)
    pairs = [
        (signal_hbm, signal),
        (gate_in_hbm, gate_in),
        (features_hbm, features),
        (pos_weight_hbm, pos_weight),
        (pos_bias_hbm, pos_bias),
        (frequency_hbm, frequency),
        (inner_weight_hbm, inner_weight),
        (inner_bias_hbm, inner_bias),
        (out_weight_hbm.at[:, mine], weight),
        (decay_rates_hbm.at[:, mine], decay),
        (forward_hbm, forward),
        (inverse_hbm, inverse),
        (gate_out_hbm, gate_out),
        (skip_gain_hbm, skip_gain),
    ]
    loads = [
        pltpu.make_async_copy(source, target, load_sem.at[index])
        for index, (source, target) in enumerate(pairs)
    ]
    for copy in loads:
        copy.start()

    for copy in loads[:2]:
        copy.wait()
    for chunk in range(chunks):
        for owner in range(blocks):
            columns = pl.ds(owner * own + chunk * LANES, LANES)
            gated[owner, chunk] = (
                gate_in[0, :, columns].astype(jnp.float32)
                * signal[0, :, columns].astype(jnp.float32)
            ).astype(jnp.bfloat16)
    pl.semaphore_wait(barrier, len(peers))

    def exchange(phase, chunk, source_of, target):
        copies = []
        for slot, peer in enumerate(peers):
            copy = pltpu.make_async_remote_copy(
                src_ref=source_of(peer),
                dst_ref=target.at[chunk, me],
                send_sem=send_sem.at[phase, chunk, slot],
                recv_sem=recv_sem.at[phase, chunk, slot],
                device_id={"seq": peer},
                device_id_type=pl.DeviceIdType.MESH,
            )
            copy.start()
            copies.append(copy)
        return copies

    incoming = [
        exchange(0, chunk, lambda peer, chunk=chunk: gated.at[peer, chunk], inbox)
        for chunk in range(chunks)
    ]
    for chunk in range(chunks):
        inbox[chunk, me] = gated[me, chunk]

    order = frequency.shape[1]
    diagonal = lax.broadcasted_iota(jnp.int32, (order, order), 0) == lax.broadcasted_iota(
        jnp.int32, (order, order), 1
    )

    def as_column(row):
        return jnp.sum(jnp.where(diagonal, row, 0.0), axis=1, keepdims=True)

    def layer(left, right, bias):
        return sine(rate * (stacked_dot(left, right) + as_column(bias)))

    for copy in loads[2:10]:
        copy.wait()
    rate = as_column(frequency[...])
    wide_weight[...] = jnp.zeros_like(wide_weight)
    wide_weight[: pos_weight.shape[0], :] = pos_weight[...]
    left = stacked(pieces(wide_weight[...], 3), LEFT_ORDER)
    hidden[...] = layer(left, features[...], pos_bias[...])
    for index in range(inner_weight.shape[0]):
        left = stacked(pieces(inner_weight[index], 3), LEFT_ORDER)
        right = stacked(pieces(hidden[...], 3), RIGHT_ORDER)
        hidden[...] = layer(left, right, inner_bias[pl.ds(index, 1), :])
    right = stacked(pieces(weight[...], 2), (0, 0, 1, 1))
    energy = jnp.zeros((1, own), jnp.float32)
    for a in range(blocks):
        place = lax.broadcasted_iota(jnp.int32, (span, own), 0) + a * span
        moment = place.astype(jnp.float32) / float(length - 1)
        left = stacked(pieces(hidden[:, a * span : (a + 1) * span], 2), (0, 1, 0, 1))
        raw = stacked_dot(left, right) * (jnp.exp(-moment * decay[...]) + FLOOR_SHIFT)
        energy = energy + jnp.sum(raw * raw, axis=0, keepdims=True)
        taps[a] = raw.astype(jnp.bfloat16)
    scale = lax.rsqrt(energy + EPSILON)

    group = 16

    def tap_section(step, carry):
        rows = pl.ds(pl.multiple_of(step * group, group), group)

        def store(c, part, value):
            tap_rows[c, part, rows, :] = value

        sections(lambda a: taps[a, rows, :], store, blocks)
        return carry

    lax.fori_loop(0, span // group, tap_section, 0)
    for copy in loads[10:12]:
        copy.wait()

    def spectrum(c, rows):
        if c in (0, blocks):
            table, data = forward[c, :, :span], rows[0]
        else:
            table, data = forward[c], jnp.concatenate([rows[0], rows[1]], axis=0)
        return jnp.dot(table, data, preferred_element_type=jnp.float32)

    for c in range(blocks + 1):
        filt[c] = spectrum(c, tap_rows.at[c]) * scale

    outgoing = []
    for chunk in range(chunks):
        for copy in incoming[chunk]:
            copy.wait_recv()

        def data_section(step, carry):
            rows = pl.ds(pl.multiple_of(step * group, group), group)

            def store(c, part, value):
                data_rows[c, part, rows, :] = value

            sections(lambda a: inbox[chunk, a, rows, :], store, blocks)
            return carry

        lax.fori_loop(0, span // group, data_section, 0)
        lanes = slice(chunk * LANES, (chunk + 1) * LANES)
        for c in range(blocks + 1):
            wave = spectrum(c, data_rows.at[c])
            wave_real, wave_imag = wave[:span], wave[span:]
            filt_real, filt_imag = filt[c, :span, lanes], filt[c, span:, lanes]
            product = jnp.concatenate(
                [
                    (wave_real * filt_real - wave_imag * filt_imag).astype(jnp.bfloat16),
                    (wave_real * filt_imag + wave_imag * filt_real).astype(jnp.bfloat16),
                ],
                axis=0,
            )
            if c in (0, blocks):
                back[c, :span] = jnp.dot(
                    inverse[c, :span, :], product, preferred_element_type=jnp.float32
                )
            else:
                back[c] = jnp.dot(inverse[c], product, preferred_element_type=jnp.float32)

        def join_section(step, carry):
            small = 8

            def load(c, part):
                return back[c, pl.ds(pl.multiple_of(part * span + step * group, small), group), :]

            def store(a, value):
                outbox[chunk, a, pl.ds(pl.multiple_of(step * group, group), group), :] = value

            joined(load, store, blocks, 1.0 / (2 * length))
            return carry

        lax.fori_loop(0, span // group, join_section, 0)
        outgoing.append(
            exchange(1, chunk, lambda peer, chunk=chunk: outbox.at[chunk, peer], returned)
        )

    def finish(chunk, slot, owner, convolved):
        columns = pl.ds(pl.multiple_of(owner * own + chunk * LANES, LANES), LANES)
        staged[0, :, columns] = (
            gate_out[0, :, columns].astype(jnp.float32)
            * (
                convolved.astype(jnp.float32)
                + skip_gain[:, columns] * gated[owner, chunk].astype(jnp.float32)
            )
        ).astype(jnp.bfloat16)
        copy = pltpu.make_async_copy(
            staged.at[:, :, columns], out.at[:, :, columns], leave_sem.at[chunk, slot]
        )
        copy.start()
        leaving.append(copy)

    leaving = []
    for copy in loads[12:]:
        copy.wait()
    for chunk in range(chunks):
        finish(chunk, 0, me, outbox[chunk, me])
    for chunk in range(chunks):
        for slot, (peer, copy) in enumerate(zip(peers, outgoing[chunk])):
            copy.wait_recv()
            finish(chunk, slot + 1, peer, returned[chunk, peer])
    for copy in leaving:
        copy.wait()
    for copies in incoming + outgoing:
        for copy in copies:
            copy.wait_send()


def settle_kernel(source, target, sem):
    parts = sem.shape[0]
    rows = source.shape[1] // parts
    copies = [
        pltpu.make_async_copy(
            source.at[:, pl.ds(part * rows, rows), :],
            target.at[:, pl.ds(part * rows, rows), :],
            sem.at[part],
        )
        for part in range(parts)
    ]
    for copy in copies:
        copy.start()
    for copy in copies:
        copy.wait()


def fused(
    signal,
    gate_in,
    gate_out,
    pos_weight,
    pos_bias,
    inner_weight,
    inner_bias,
    frequency,
    out_weight,
    decay_rates,
    skip_gain,
):
    blocks = lax.axis_size("seq")
    span, width = signal.shape[1], signal.shape[2]
    own = width // blocks
    chunks = own // LANES
    length = span * blocks
    order = frequency.shape[0]
    forward, inverse = row_matrices(blocks, span)
    features = position_features(length, pos_weight.shape[0])
    hbm = pl.BlockSpec(memory_space=pltpu.HBM)
    bf16, f32 = jnp.bfloat16, jnp.float32
    operands = (
        signal,
        gate_in,
        gate_out,
        jnp.asarray(features),
        pos_weight,
        pos_bias.reshape(1, -1),
        inner_weight,
        inner_bias,
        frequency.reshape(1, -1),
        out_weight,
        decay_rates.reshape(1, -1),
        skip_gain.reshape(1, -1),
        jnp.asarray(forward),
        jnp.asarray(inverse),
    )
    shapes = [operand.shape for operand in operands]
    shapes[9], shapes[10] = (order, own), (1, own)
    locals_ = [pltpu.VMEM(shape, operand.dtype) for shape, operand in zip(shapes, operands)]
    mixed = pl.pallas_call(
        functools.partial(layer_kernel, blocks, span, own),
        out_shape=jax.ShapeDtypeStruct(signal.shape, bf16),
        in_specs=[hbm] * len(operands),
        out_specs=hbm,
        scratch_shapes=[
            *locals_,
            pltpu.VMEM(signal.shape, bf16),
            pltpu.VMEM((padded(pos_weight.shape[0]), order), f32),
            pltpu.VMEM((blocks, chunks, span, LANES), bf16),
            pltpu.VMEM((chunks, blocks, span, LANES), bf16),
            pltpu.VMEM((chunks, blocks, span, LANES), bf16),
            pltpu.VMEM((chunks, blocks, span, LANES), bf16),
            pltpu.VMEM((order, length), f32),
            pltpu.VMEM((blocks, span, own), bf16),
            pltpu.VMEM((blocks + 1, 2, span, own), bf16),
            pltpu.VMEM((blocks + 1, 2 * span, own), f32),
            pltpu.VMEM((blocks + 1, 2, span, LANES), bf16),
            pltpu.VMEM((blocks + 1, 2 * span, LANES), f32),
            pltpu.SemaphoreType.DMA((len(operands),)),
            pltpu.SemaphoreType.DMA((chunks, blocks)),
            pltpu.SemaphoreType.DMA((2, chunks, blocks)),
            pltpu.SemaphoreType.DMA((2, chunks, blocks)),
        ],
        compiler_params=pltpu.CompilerParams(
            collective_id=0, has_side_effects=True, vmem_limit_bytes=62 * MIB
        ),
        name="hyena_layer",
    )(*operands)
    return pl.pallas_call(
        settle_kernel,
        out_shape=jax.ShapeDtypeStruct(mixed.shape, bf16),
        in_specs=[hbm],
        out_specs=hbm,
        scratch_shapes=[pltpu.SemaphoreType.DMA((blocks,))],
        compiler_params=pltpu.CompilerParams(vmem_limit_bytes=62 * MIB),
        name="settle",
    )(mixed)


def unit_angle(index, period):
    return (index % period).astype(jnp.float32) * (TWO_PI / period)


def section_tables(row_ids, col_ids, period):
    angle = unit_angle(row_ids[:, None] * col_ids[None, :], period)
    return (jnp.cos(angle).astype(jnp.bfloat16), jnp.sin(angle).astype(jnp.bfloat16))


def filter_hidden(positions, total, pos_weight, pos_bias, inner_weight, inner_bias, frequency):
    band_count = (pos_weight.shape[0] - 1) // 2
    position_f = positions.astype(jnp.float32)
    moments = position_f / (total - 1)
    phases = position_f * (TWO_PI / total)
    tone_list = jnp.linspace(0.0001, band_count - 1, band_count).astype(jnp.float32)
    angles = tone_list[:, None] * phases[None, :]
    features = jnp.concatenate([moments[None, :], jnp.cos(angles), -jnp.sin(angles)], axis=0)
    hidden = jnp.sin(
        frequency[:, None]
        * (jnp.dot(pos_weight.T, features, precision=HIGHEST) + pos_bias[:, None])
    )
    for layer_index in range(inner_weight.shape[0]):
        hidden = jnp.sin(
            frequency[:, None]
            * (
                jnp.dot(inner_weight[layer_index].T, hidden, precision=HIGHEST)
                + inner_bias[layer_index][:, None]
            )
        )
    return (hidden, moments)


def plain(
    signal,
    gate_in,
    gate_out,
    pos_weight,
    pos_bias,
    inner_weight,
    inner_bias,
    frequency,
    out_weight,
    decay_rates,
    skip_gain,
):
    blocks = lax.axis_size("seq")
    block_id = lax.axis_index("seq")
    span = signal.shape[1]
    width = signal.shape[2]
    rows_freq = 2 * blocks
    length = span * blocks
    period = 2 * length
    gated = (gate_in[0].astype(jnp.float32) * signal[0].astype(jnp.float32)).astype(jnp.bfloat16)
    fwd_cos, fwd_sin = section_tables(
        jnp.arange(rows_freq, dtype=jnp.int32), jnp.arange(blocks, dtype=jnp.int32), rows_freq
    )
    back_cos, back_sin = section_tables(
        jnp.arange(blocks, dtype=jnp.int32), jnp.arange(rows_freq, dtype=jnp.int32), rows_freq
    )
    column_ids = jnp.arange(span, dtype=jnp.int32)
    own = width // blocks
    lanes = lax.all_to_all(gated.T, "seq", split_axis=0, concat_axis=1, tiled=True)
    own_weight = lax.dynamic_slice_in_dim(out_weight, block_id * own, own, 1)
    own_decay = lax.dynamic_slice_in_dim(decay_rates, block_id * own, own, 0)
    hidden, moments = filter_hidden(
        jnp.arange(length, dtype=jnp.int32),
        length,
        pos_weight,
        pos_bias,
        inner_weight,
        inner_bias,
        frequency,
    )
    shaped = jnp.dot(own_weight.T, hidden, precision=HIGHEST) * (
        jnp.exp(-own_decay[:, None] * moments[None, :]) + FLOOR_SHIFT
    )
    own_scale = lax.rsqrt(jnp.sum(shaped * shaped, axis=1) + EPSILON)
    own_taps = shaped.astype(jnp.bfloat16)

    def first_local(source):
        cube = source.reshape(own, blocks, span)
        real_part = jnp.einsum(
            "ca,oab->cob", fwd_cos, cube, preferred_element_type=jnp.float32
        ).astype(jnp.bfloat16)
        imag_part = (
            -jnp.einsum("ca,oab->cob", fwd_sin, cube, preferred_element_type=jnp.float32)
        ).astype(jnp.bfloat16)
        return (real_part, imag_part)

    data_real, data_imag = first_local(lanes)
    taps_real, taps_imag = first_local(own_taps)
    group = 16
    turns = rows_freq // group

    def grouped(array):
        return array.reshape(turns, group, own, span)

    def row_group(pieces):
        row_real, row_imag, tap_real, tap_imag, row_ids = pieces
        wave_ids = row_ids[:, None] + rows_freq * column_ids[None, :]
        angle = unit_angle(wave_ids[:, :, None] * column_ids[None, None, :], period)
        cosines = jnp.cos(angle).astype(jnp.bfloat16)
        sines = jnp.sin(angle).astype(jnp.bfloat16)

        def spectrum_of(part_real, part_imag):
            spec_real = jnp.einsum(
                "rdb,rob->rod", cosines, part_real, preferred_element_type=jnp.float32
            ) + jnp.einsum("rdb,rob->rod", sines, part_imag, preferred_element_type=jnp.float32)
            spec_imag = jnp.einsum(
                "rdb,rob->rod", cosines, part_imag, preferred_element_type=jnp.float32
            ) - jnp.einsum("rdb,rob->rod", sines, part_real, preferred_element_type=jnp.float32)
            return (spec_real, spec_imag)

        wave_real, wave_imag = spectrum_of(row_real, row_imag)
        spec_real, spec_imag = spectrum_of(tap_real, tap_imag)
        filt_real = spec_real.astype(jnp.bfloat16).astype(jnp.float32)
        filt_imag = spec_imag.astype(jnp.bfloat16).astype(jnp.float32)
        lane_scale = own_scale[None, :, None]
        prod_real = ((wave_real * filt_real - wave_imag * filt_imag) * lane_scale).astype(
            jnp.bfloat16
        )
        prod_imag = ((wave_real * filt_imag + wave_imag * filt_real) * lane_scale).astype(
            jnp.bfloat16
        )
        back_real = jnp.einsum(
            "rdb,rod->rob", cosines, prod_real, preferred_element_type=jnp.float32
        ) - jnp.einsum("rdb,rod->rob", sines, prod_imag, preferred_element_type=jnp.float32)
        back_imag = jnp.einsum(
            "rdb,rod->rob", cosines, prod_imag, preferred_element_type=jnp.float32
        ) + jnp.einsum("rdb,rod->rob", sines, prod_real, preferred_element_type=jnp.float32)
        return (back_real.astype(jnp.bfloat16), back_imag.astype(jnp.bfloat16))

    row_list = jnp.arange(rows_freq, dtype=jnp.int32).reshape(turns, group)
    back_real, back_imag = lax.map(
        row_group,
        (grouped(data_real), grouped(data_imag), grouped(taps_real), grouped(taps_imag), row_list),
    )
    back_real = back_real.reshape(rows_freq, own, span)
    back_imag = back_imag.reshape(rows_freq, own, span)
    local_conv = (
        jnp.einsum("ac,cob->oab", back_cos, back_real, preferred_element_type=jnp.float32)
        - jnp.einsum("ac,cob->oab", back_sin, back_imag, preferred_element_type=jnp.float32)
    ) * (1.0 / period)
    returned = lax.all_to_all(
        local_conv.reshape(own, length).astype(jnp.bfloat16),
        "seq",
        split_axis=1,
        concat_axis=0,
        tiled=True,
    ).astype(jnp.float32)
    convolved_rows = returned.T
    mixed = gate_out[0].astype(jnp.float32) * (
        convolved_rows + skip_gain[None, :] * gated.astype(jnp.float32)
    )
    return mixed.astype(jnp.bfloat16)[None]


def fits_kernel(blocks, span, width):
    own = width // blocks
    power = blocks >= 4 and blocks & (blocks - 1) == 0
    return power and span == LANES and own > 0 and own % LANES == 0


def per_device(signal, *rest):
    if fits_kernel(lax.axis_size("seq"), signal.shape[1], signal.shape[2]):
        return fused(signal, *rest)
    return plain(signal, *rest)


def solution(mesh):
    return jax.shard_map(
        per_device,
        mesh=mesh,
        in_specs=(
            P("grp", "seq", None),
            P("grp", "seq", None),
            P("grp", "seq", None),
            P(),
            P(),
            P(),
            P(),
            P(),
            P(),
            P(),
            P(),
        ),
        out_specs=P("grp", "seq", None),
        check_vma=False,
    )
```

```python
import functools
import math

import jax
import jax.numpy as jnp
import ml_dtypes
import numpy as np
from jax import lax
from jax.experimental import pallas as pl
from jax.experimental.pallas import tpu as pltpu
from jax.sharding import PartitionSpec as P

TWO_PI = 6.283185307179586
FLOOR_SHIFT = 0.05
EPSILON = 1e-06
HIGHEST = lax.Precision.HIGHEST
LANES = 128
MIB = 1024 * 1024


def row_matrices(blocks, span):
    rows_freq = 2 * blocks
    period = rows_freq * span
    ids = np.arange(span, dtype=np.int64)
    wave = np.arange(blocks + 1)[:, None] + rows_freq * ids[None, :]
    turns = (wave[:, :, None] * ids[None, None, :]) % period
    angle = turns.astype(np.float32) * np.float32(TWO_PI / period)
    cosines, sines = np.cos(angle), np.sin(angle)
    upper = np.concatenate([cosines, sines], axis=2)
    lower = np.concatenate([-sines, cosines], axis=2)
    forward = np.concatenate([upper, lower], axis=1).astype(ml_dtypes.bfloat16)
    return forward, np.ascontiguousarray(forward.transpose(0, 2, 1))


def padded(rows):
    return -(-rows // 8) * 8


def position_features(length, emb):
    band_count = (emb - 1) // 2
    position_f = np.arange(length, dtype=np.float32)
    moments = position_f / np.float32(length - 1)
    phases = position_f * np.float32(TWO_PI / length)
    tones = np.linspace(0.0001, band_count - 1, band_count).astype(np.float32)
    angles = tones[:, None] * phases[None, :]
    features = np.concatenate([moments[None, :], np.cos(angles), -np.sin(angles)], axis=0)
    rest = np.pad(features, ((0, padded(emb) - emb), (0, 0)))
    parts = []
    for _ in range(3):
        parts.append(rest.astype(ml_dtypes.bfloat16).astype(np.float32))
        rest = rest - parts[-1]
    rows = np.concatenate([parts[index] for index in RIGHT_ORDER], axis=0)
    return rows.astype(ml_dtypes.bfloat16)


def sine(value):
    turns = jnp.round(value * (1.0 / math.pi))
    rest = value - turns * 3.140625
    rest = rest - turns * 9.67502593994140625e-4
    rest = rest - turns * 1.509957990978376432e-7
    parity = turns - 2.0 * jnp.floor(turns * 0.5)
    square = rest * rest
    poly = -2.3889859e-08 * square + 2.7525562e-06
    poly = poly * square - 0.00019840874
    poly = poly * square + 0.0083333310
    poly = poly * square - 0.16666667
    signed = rest - 2.0 * parity * rest
    return signed + signed * (square * poly)


def pieces(value, count):
    parts = []
    for _ in range(count):
        part = value.astype(jnp.bfloat16).astype(jnp.float32)
        parts.append(part)
        value = value - part
    return parts


LEFT_ORDER, RIGHT_ORDER = (0, 1, 0, 1, 0, 2), (0, 0, 1, 1, 2, 0)


def stacked(parts, order):
    return jnp.concatenate([parts[index] for index in order], axis=0).astype(jnp.bfloat16)


def stacked_dot(left, right):
    return lax.dot_general(
        left, right, (((0,), (0,)), ((), ())), preferred_element_type=jnp.float32
    )


def weighted(terms):
    total = None
    for factor, value in terms:
        if abs(factor) < 1e-9:
            continue
        if abs(factor - 1.0) < 1e-9:
            total = value if total is None else total + value
        elif abs(factor + 1.0) < 1e-9:
            total = -value if total is None else total - value
        else:
            part = value * factor
            total = part if total is None else total + part
    return total


def sections(load, store, blocks):
    half = blocks // 2
    x = [load(a).astype(jnp.float32) for a in range(blocks)]
    plus = {a: x[a] + x[blocks - a] for a in range(1, half)}
    minus = {a: x[a] - x[blocks - a] for a in range(1, half)}
    for c in range(blocks + 1):
        step = math.pi * c / blocks
        even = c % 2 == 0
        on_cos, on_sin = (plus, minus) if even else (minus, plus)
        middle = [(math.cos(step * half), x[half])] if even else []
        real = weighted([(1.0, x[0])] + middle + [(math.cos(step * a), on_cos[a]) for a in on_cos])
        store(c, 0, real.astype(jnp.bfloat16))
        if 0 < c < blocks:
            middle = [] if even else [(-math.sin(step * half), x[half])]
            imag = weighted(middle + [(-math.sin(step * a), on_sin[a]) for a in on_sin])
            store(c, 1, imag.astype(jnp.bfloat16))


def joined(load, store, blocks, factor):
    half = blocks // 2
    real = [load(c, 0) * (factor if c in (0, blocks) else 2.0 * factor) for c in range(blocks + 1)]
    imag = {c: load(c, 1) * (2.0 * factor) for c in range(1, blocks)}
    for a in range(half + 1):
        step = math.pi * a / blocks
        even_cos = weighted([(math.cos(step * c), real[c]) for c in range(0, blocks + 1, 2)])
        odd_cos = weighted([(math.cos(step * c), real[c]) for c in range(1, blocks + 1, 2)])
        even_sin = weighted([(math.sin(step * c), imag[c]) for c in range(2, blocks, 2)])
        odd_sin = weighted([(math.sin(step * c), imag[c]) for c in range(1, blocks, 2)])
        both = even_cos if odd_sin is None else even_cos - odd_sin
        turn = None
        if odd_cos is not None and even_sin is not None:
            turn = odd_cos - even_sin
        elif odd_cos is not None:
            turn = odd_cos
        elif even_sin is not None:
            turn = -even_sin
        store(a, (both if turn is None else both + turn).astype(jnp.bfloat16))
        if 0 < a < half:
            store(blocks - a, (both if turn is None else both - turn).astype(jnp.bfloat16))


def partner(me, mask, count):
    total, bit = 0, 1
    while bit < count:
        digit = (me // bit) % 2
        total = total + bit * ((1 - digit) if mask & bit else digit)
        bit *= 2
    return total


def layer_kernel(
    blocks,
    span,
    own,
    signal_hbm,
    gate_in_hbm,
    gate_out_hbm,
    features_hbm,
    pos_weight_hbm,
    pos_bias_hbm,
    inner_weight_hbm,
    inner_bias_hbm,
    frequency_hbm,
    out_weight_hbm,
    decay_rates_hbm,
    skip_gain_hbm,
    forward_hbm,
    inverse_hbm,
    out,
    signal,
    gate_in,
    gate_out,
    features,
    pos_weight,
    pos_bias,
    inner_weight,
    inner_bias,
    frequency,
    weight,
    decay,
    skip_gain,
    forward,
    inverse,
    staged,
    wide_weight,
    gated,
    inbox,
    outbox,
    returned,
    hidden,
    taps,
    tap_rows,
    filt,
    data_rows,
    back,
    load_sem,
    leave_sem,
    send_sem,
    recv_sem,
):
    me = lax.axis_index("seq")
    chunks = own // LANES
    length = blocks * span
    masks = list(range(blocks - 1, 0, -1))
    peers = {mask: partner(me, mask, blocks) for mask in masks}

    barrier = pltpu.get_barrier_semaphore()
    for mask in masks:
        pl.semaphore_signal(
            barrier, inc=1, device_id={"seq": peers[mask]}, device_id_type=pl.DeviceIdType.MESH
        )
    mine = pl.ds(pl.multiple_of(me * own, LANES), own)
    pairs = [
        (signal_hbm, signal),
        (gate_in_hbm, gate_in),
        (features_hbm, features),
        (pos_weight_hbm, pos_weight),
        (pos_bias_hbm, pos_bias),
        (frequency_hbm, frequency),
        (inner_weight_hbm, inner_weight),
        (inner_bias_hbm, inner_bias),
        (out_weight_hbm.at[:, mine], weight),
        (decay_rates_hbm.at[:, mine], decay),
        (forward_hbm, forward),
        (inverse_hbm, inverse),
        (gate_out_hbm, gate_out),
        (skip_gain_hbm, skip_gain),
    ]
    loads = [
        pltpu.make_async_copy(source, target, load_sem.at[index])
        for index, (source, target) in enumerate(pairs)
    ]
    for copy in loads:
        copy.start()

    for copy in loads[:2]:
        copy.wait()
    def gate(chunk):
        for owner in range(blocks):
            columns = pl.ds(owner * own + chunk * LANES, LANES)
            gated[owner, chunk] = (
                gate_in[0, :, columns].astype(jnp.float32)
                * signal[0, :, columns].astype(jnp.float32)
            ).astype(jnp.bfloat16)
        inbox[chunk, me] = gated[me, chunk]

    gate(0)
    pl.semaphore_wait(barrier, len(masks))

    def exchange(phase, chunk, source_of, target):
        copies = []
        for mask in masks:
            copy = pltpu.make_async_remote_copy(
                src_ref=source_of(peers[mask]),
                dst_ref=target.at[chunk, me],
                send_sem=send_sem.at[phase, chunk, mask],
                recv_sem=recv_sem.at[phase, chunk, mask],
                device_id={"seq": peers[mask]},
                device_id_type=pl.DeviceIdType.MESH,
            )
            copy.start()
            copies.append(copy)
        return copies

    def depart(chunk):
        return exchange(0, chunk, lambda peer: gated.at[peer, chunk], inbox)

    incoming = [depart(0)]
    for chunk in range(1, chunks):
        gate(chunk)

    order = frequency.shape[1]
    diagonal = lax.broadcasted_iota(jnp.int32, (order, order), 0) == lax.broadcasted_iota(
        jnp.int32, (order, order), 1
    )

    def as_column(row):
        return jnp.sum(jnp.where(diagonal, row, 0.0), axis=1, keepdims=True)

    def layer(left, right, bias):
        return sine(rate * (stacked_dot(left, right) + as_column(bias)))

    for copy in loads[2:10]:
        copy.wait()
    rate = as_column(frequency[...])
    wide_weight[...] = jnp.zeros_like(wide_weight)
    wide_weight[: pos_weight.shape[0], :] = pos_weight[...]
    left = stacked(pieces(wide_weight[...], 3), LEFT_ORDER)
    hidden[...] = layer(left, features[...], pos_bias[...])
    for index in range(inner_weight.shape[0]):
        left = stacked(pieces(inner_weight[index], 3), LEFT_ORDER)
        right = stacked(pieces(hidden[...], 3), RIGHT_ORDER)
        hidden[...] = layer(left, right, inner_bias[pl.ds(index, 1), :])
    right = stacked(pieces(weight[...], 2), (0, 0, 1, 1))
    energy = jnp.zeros((1, own), jnp.float32)
    for a in range(blocks):
        place = lax.broadcasted_iota(jnp.int32, (span, own), 0) + a * span
        moment = place.astype(jnp.float32) / float(length - 1)
        left = stacked(pieces(hidden[:, a * span : (a + 1) * span], 2), (0, 1, 0, 1))
        raw = stacked_dot(left, right) * (jnp.exp(-moment * decay[...]) + FLOOR_SHIFT)
        energy = energy + jnp.sum(raw * raw, axis=0, keepdims=True)
        taps[a] = raw.astype(jnp.bfloat16)
    scale = lax.rsqrt(energy + EPSILON)

    for chunk in range(1, chunks):
        for copy in incoming[chunk - 1]:
            copy.wait_send()
        incoming.append(depart(chunk))

    group = 16

    def tap_section(step, carry):
        rows = pl.ds(pl.multiple_of(step * group, group), group)

        def store(c, part, value):
            tap_rows[c, part, rows, :] = value

        sections(lambda a: taps[a, rows, :], store, blocks)
        return carry

    lax.fori_loop(0, span // group, tap_section, 0)
    for copy in loads[10:12]:
        copy.wait()

    def spectrum(c, rows):
        if c in (0, blocks):
            table, data = forward[c, :, :span], rows[0]
        else:
            table, data = forward[c], jnp.concatenate([rows[0], rows[1]], axis=0)
        return jnp.dot(table, data, preferred_element_type=jnp.float32)

    for c in range(blocks + 1):
        filt[c] = spectrum(c, tap_rows.at[c]) * scale

    outgoing = []
    for chunk in range(chunks):
        for copy in incoming[chunk]:
            copy.wait_recv()

        def data_section(step, carry):
            rows = pl.ds(pl.multiple_of(step * group, group), group)

            def store(c, part, value):
                data_rows[c, part, rows, :] = value

            sections(lambda a: inbox[chunk, a, rows, :], store, blocks)
            return carry

        lax.fori_loop(0, span // group, data_section, 0)
        lanes = slice(chunk * LANES, (chunk + 1) * LANES)
        for c in range(blocks + 1):
            wave = spectrum(c, data_rows.at[c])
            wave_real, wave_imag = wave[:span], wave[span:]
            filt_real, filt_imag = filt[c, :span, lanes], filt[c, span:, lanes]
            product = jnp.concatenate(
                [
                    (wave_real * filt_real - wave_imag * filt_imag).astype(jnp.bfloat16),
                    (wave_real * filt_imag + wave_imag * filt_real).astype(jnp.bfloat16),
                ],
                axis=0,
            )
            if c in (0, blocks):
                back[c, :span] = jnp.dot(
                    inverse[c, :span, :], product, preferred_element_type=jnp.float32
                )
            else:
                back[c] = jnp.dot(inverse[c], product, preferred_element_type=jnp.float32)

        def join_section(step, carry):
            small = 8

            def load(c, part):
                return back[c, pl.ds(pl.multiple_of(part * span + step * group, small), group), :]

            def store(a, value):
                outbox[chunk, a, pl.ds(pl.multiple_of(step * group, group), group), :] = value

            joined(load, store, blocks, 1.0 / (2 * length))
            return carry

        lax.fori_loop(0, span // group, join_section, 0)
        outgoing.append(
            exchange(1, chunk, lambda peer, chunk=chunk: outbox.at[chunk, peer], returned)
        )

    def finish(chunk, slot, owner, convolved):
        columns = pl.ds(pl.multiple_of(owner * own + chunk * LANES, LANES), LANES)
        staged[0, :, columns] = (
            gate_out[0, :, columns].astype(jnp.float32)
            * (
                convolved.astype(jnp.float32)
                + skip_gain[:, columns] * gated[owner, chunk].astype(jnp.float32)
            )
        ).astype(jnp.bfloat16)
        copy = pltpu.make_async_copy(
            staged.at[:, :, columns], out.at[:, :, columns], leave_sem.at[chunk, slot]
        )
        copy.start()
        leaving.append(copy)

    leaving = []
    for copy in loads[12:]:
        copy.wait()
    for chunk in range(chunks):
        finish(chunk, 0, me, outbox[chunk, me])
    for chunk in range(chunks):
        for mask, copy in reversed(list(zip(masks, outgoing[chunk]))):
            copy.wait_recv()
            finish(chunk, mask, peers[mask], returned[chunk, peers[mask]])
    for copy in leaving:
        copy.wait()
    for copies in incoming[-1:] + outgoing:
        for copy in copies:
            copy.wait_send()


def fused(
    signal,
    gate_in,
    gate_out,
    pos_weight,
    pos_bias,
    inner_weight,
    inner_bias,
    frequency,
    out_weight,
    decay_rates,
    skip_gain,
):
    blocks = lax.axis_size("seq")
    span, width = signal.shape[1], signal.shape[2]
    own = width // blocks
    chunks = own // LANES
    length = span * blocks
    order = frequency.shape[0]
    forward, inverse = row_matrices(blocks, span)
    features = position_features(length, pos_weight.shape[0])
    hbm = pl.BlockSpec(memory_space=pltpu.HBM)
    bf16, f32 = jnp.bfloat16, jnp.float32
    operands = (
        signal,
        gate_in,
        gate_out,
        jnp.asarray(features),
        pos_weight,
        pos_bias.reshape(1, -1),
        inner_weight,
        inner_bias,
        frequency.reshape(1, -1),
        out_weight,
        decay_rates.reshape(1, -1),
        skip_gain.reshape(1, -1),
        jnp.asarray(forward),
        jnp.asarray(inverse),
    )
    shapes = [operand.shape for operand in operands]
    shapes[9], shapes[10] = (order, own), (1, own)
    locals_ = [pltpu.VMEM(shape, operand.dtype) for shape, operand in zip(shapes, operands)]
    return pl.pallas_call(
        functools.partial(layer_kernel, blocks, span, own),
        out_shape=jax.ShapeDtypeStruct(signal.shape, bf16),
        in_specs=[hbm] * len(operands),
        out_specs=hbm,
        scratch_shapes=[
            *locals_,
            pltpu.VMEM(signal.shape, bf16),
            pltpu.VMEM((padded(pos_weight.shape[0]), order), f32),
            pltpu.VMEM((blocks, chunks, span, LANES), bf16),
            pltpu.VMEM((chunks, blocks, span, LANES), bf16),
            pltpu.VMEM((chunks, blocks, span, LANES), bf16),
            pltpu.VMEM((chunks, blocks, span, LANES), bf16),
            pltpu.VMEM((order, length), f32),
            pltpu.VMEM((blocks, span, own), bf16),
            pltpu.VMEM((blocks + 1, 2, span, own), bf16),
            pltpu.VMEM((blocks + 1, 2 * span, own), f32),
            pltpu.VMEM((blocks + 1, 2, span, LANES), bf16),
            pltpu.VMEM((blocks + 1, 2 * span, LANES), f32),
            pltpu.SemaphoreType.DMA((len(operands),)),
            pltpu.SemaphoreType.DMA((chunks, blocks)),
            pltpu.SemaphoreType.DMA((2, chunks, blocks)),
            pltpu.SemaphoreType.DMA((2, chunks, blocks)),
        ],
        compiler_params=pltpu.CompilerParams(
            collective_id=0, has_side_effects=True, vmem_limit_bytes=62 * MIB
        ),
        name="hyena_layer",
    )(*operands)


def unit_angle(index, period):
    return (index % period).astype(jnp.float32) * (TWO_PI / period)


def section_tables(row_ids, col_ids, period):
    angle = unit_angle(row_ids[:, None] * col_ids[None, :], period)
    return (jnp.cos(angle).astype(jnp.bfloat16), jnp.sin(angle).astype(jnp.bfloat16))


def filter_hidden(positions, total, pos_weight, pos_bias, inner_weight, inner_bias, frequency):
    band_count = (pos_weight.shape[0] - 1) // 2
    position_f = positions.astype(jnp.float32)
    moments = position_f / (total - 1)
    phases = position_f * (TWO_PI / total)
    tone_list = jnp.linspace(0.0001, band_count - 1, band_count).astype(jnp.float32)
    angles = tone_list[:, None] * phases[None, :]
    features = jnp.concatenate([moments[None, :], jnp.cos(angles), -jnp.sin(angles)], axis=0)
    hidden = jnp.sin(
        frequency[:, None]
        * (jnp.dot(pos_weight.T, features, precision=HIGHEST) + pos_bias[:, None])
    )
    for layer_index in range(inner_weight.shape[0]):
        hidden = jnp.sin(
            frequency[:, None]
            * (
                jnp.dot(inner_weight[layer_index].T, hidden, precision=HIGHEST)
                + inner_bias[layer_index][:, None]
            )
        )
    return (hidden, moments)


def plain(
    signal,
    gate_in,
    gate_out,
    pos_weight,
    pos_bias,
    inner_weight,
    inner_bias,
    frequency,
    out_weight,
    decay_rates,
    skip_gain,
):
    blocks = lax.axis_size("seq")
    block_id = lax.axis_index("seq")
    span = signal.shape[1]
    width = signal.shape[2]
    rows_freq = 2 * blocks
    length = span * blocks
    period = 2 * length
    gated = (gate_in[0].astype(jnp.float32) * signal[0].astype(jnp.float32)).astype(jnp.bfloat16)
    fwd_cos, fwd_sin = section_tables(
        jnp.arange(rows_freq, dtype=jnp.int32), jnp.arange(blocks, dtype=jnp.int32), rows_freq
    )
    back_cos, back_sin = section_tables(
        jnp.arange(blocks, dtype=jnp.int32), jnp.arange(rows_freq, dtype=jnp.int32), rows_freq
    )
    column_ids = jnp.arange(span, dtype=jnp.int32)
    own = width // blocks
    lanes = lax.all_to_all(gated.T, "seq", split_axis=0, concat_axis=1, tiled=True)
    own_weight = lax.dynamic_slice_in_dim(out_weight, block_id * own, own, 1)
    own_decay = lax.dynamic_slice_in_dim(decay_rates, block_id * own, own, 0)
    hidden, moments = filter_hidden(
        jnp.arange(length, dtype=jnp.int32),
        length,
        pos_weight,
        pos_bias,
        inner_weight,
        inner_bias,
        frequency,
    )
    shaped = jnp.dot(own_weight.T, hidden, precision=HIGHEST) * (
        jnp.exp(-own_decay[:, None] * moments[None, :]) + FLOOR_SHIFT
    )
    own_scale = lax.rsqrt(jnp.sum(shaped * shaped, axis=1) + EPSILON)
    own_taps = shaped.astype(jnp.bfloat16)

    def first_local(source):
        cube = source.reshape(own, blocks, span)
        real_part = jnp.einsum(
            "ca,oab->cob", fwd_cos, cube, preferred_element_type=jnp.float32
        ).astype(jnp.bfloat16)
        imag_part = (
            -jnp.einsum("ca,oab->cob", fwd_sin, cube, preferred_element_type=jnp.float32)
        ).astype(jnp.bfloat16)
        return (real_part, imag_part)

    data_real, data_imag = first_local(lanes)
    taps_real, taps_imag = first_local(own_taps)
    group = 16
    turns = rows_freq // group

    def grouped(array):
        return array.reshape(turns, group, own, span)

    def row_group(pieces):
        row_real, row_imag, tap_real, tap_imag, row_ids = pieces
        wave_ids = row_ids[:, None] + rows_freq * column_ids[None, :]
        angle = unit_angle(wave_ids[:, :, None] * column_ids[None, None, :], period)
        cosines = jnp.cos(angle).astype(jnp.bfloat16)
        sines = jnp.sin(angle).astype(jnp.bfloat16)

        def spectrum_of(part_real, part_imag):
            spec_real = jnp.einsum(
                "rdb,rob->rod", cosines, part_real, preferred_element_type=jnp.float32
            ) + jnp.einsum("rdb,rob->rod", sines, part_imag, preferred_element_type=jnp.float32)
            spec_imag = jnp.einsum(
                "rdb,rob->rod", cosines, part_imag, preferred_element_type=jnp.float32
            ) - jnp.einsum("rdb,rob->rod", sines, part_real, preferred_element_type=jnp.float32)
            return (spec_real, spec_imag)

        wave_real, wave_imag = spectrum_of(row_real, row_imag)
        spec_real, spec_imag = spectrum_of(tap_real, tap_imag)
        filt_real = spec_real.astype(jnp.bfloat16).astype(jnp.float32)
        filt_imag = spec_imag.astype(jnp.bfloat16).astype(jnp.float32)
        lane_scale = own_scale[None, :, None]
        prod_real = ((wave_real * filt_real - wave_imag * filt_imag) * lane_scale).astype(
            jnp.bfloat16
        )
        prod_imag = ((wave_real * filt_imag + wave_imag * filt_real) * lane_scale).astype(
            jnp.bfloat16
        )
        back_real = jnp.einsum(
            "rdb,rod->rob", cosines, prod_real, preferred_element_type=jnp.float32
        ) - jnp.einsum("rdb,rod->rob", sines, prod_imag, preferred_element_type=jnp.float32)
        back_imag = jnp.einsum(
            "rdb,rod->rob", cosines, prod_imag, preferred_element_type=jnp.float32
        ) + jnp.einsum("rdb,rod->rob", sines, prod_real, preferred_element_type=jnp.float32)
        return (back_real.astype(jnp.bfloat16), back_imag.astype(jnp.bfloat16))

    row_list = jnp.arange(rows_freq, dtype=jnp.int32).reshape(turns, group)
    back_real, back_imag = lax.map(
        row_group,
        (grouped(data_real), grouped(data_imag), grouped(taps_real), grouped(taps_imag), row_list),
    )
    back_real = back_real.reshape(rows_freq, own, span)
    back_imag = back_imag.reshape(rows_freq, own, span)
    local_conv = (
        jnp.einsum("ac,cob->oab", back_cos, back_real, preferred_element_type=jnp.float32)
        - jnp.einsum("ac,cob->oab", back_sin, back_imag, preferred_element_type=jnp.float32)
    ) * (1.0 / period)
    returned = lax.all_to_all(
        local_conv.reshape(own, length).astype(jnp.bfloat16),
        "seq",
        split_axis=1,
        concat_axis=0,
        tiled=True,
    ).astype(jnp.float32)
    convolved_rows = returned.T
    mixed = gate_out[0].astype(jnp.float32) * (
        convolved_rows + skip_gain[None, :] * gated.astype(jnp.float32)
    )
    return mixed.astype(jnp.bfloat16)[None]


def fits_kernel(blocks, span, width):
    own = width // blocks
    power = blocks >= 4 and blocks & (blocks - 1) == 0
    return power and span == LANES and own > 0 and own % LANES == 0


def per_device(signal, *rest):
    if fits_kernel(lax.axis_size("seq"), signal.shape[1], signal.shape[2]):
        return fused(signal, *rest)
    return plain(signal, *rest)


def solution(mesh):
    return jax.shard_map(
        per_device,
        mesh=mesh,
        in_specs=(
            P("grp", "seq", None),
            P("grp", "seq", None),
            P("grp", "seq", None),
            P(),
            P(),
            P(),
            P(),
            P(),
            P(),
            P(),
            P(),
        ),
        out_specs=P("grp", "seq", None),
        check_vma=False,
    )
```

```python
import functools
import math

import jax
import jax.numpy as jnp
import ml_dtypes
import numpy as np
from jax import lax
from jax.experimental import pallas as pl
from jax.experimental.pallas import tpu as pltpu
from jax.sharding import PartitionSpec as P

TWO_PI = 6.283185307179586
FLOOR_SHIFT = 0.05
EPSILON = 1e-06
HIGHEST = lax.Precision.HIGHEST
LANES = 128
MIB = 1024 * 1024


def row_matrices(blocks, span):
    rows_freq = 2 * blocks
    period = rows_freq * span
    ids = np.arange(span, dtype=np.int64)
    wave = np.arange(blocks + 1)[:, None] + rows_freq * ids[None, :]
    turns = (wave[:, :, None] * ids[None, None, :]) % period
    angle = turns.astype(np.float32) * np.float32(TWO_PI / period)
    cosines, sines = np.cos(angle), np.sin(angle)
    upper = np.concatenate([cosines, sines], axis=2)
    lower = np.concatenate([-sines, cosines], axis=2)
    forward = np.concatenate([upper, lower], axis=1).astype(ml_dtypes.bfloat16)
    return forward, np.ascontiguousarray(forward.transpose(0, 2, 1))


def padded(rows):
    return -(-rows // 8) * 8


def position_features(length, emb):
    band_count = (emb - 1) // 2
    position_f = np.arange(length, dtype=np.float32)
    moments = position_f / np.float32(length - 1)
    phases = position_f * np.float32(TWO_PI / length)
    tones = np.linspace(0.0001, band_count - 1, band_count).astype(np.float32)
    angles = tones[:, None] * phases[None, :]
    features = np.concatenate([moments[None, :], np.cos(angles), -np.sin(angles)], axis=0)
    rest = np.pad(features, ((0, padded(emb) - emb), (0, 0)))
    parts = []
    for _ in range(3):
        parts.append(rest.astype(ml_dtypes.bfloat16).astype(np.float32))
        rest = rest - parts[-1]
    rows = np.concatenate([parts[index] for index in RIGHT_ORDER], axis=0)
    return rows.astype(ml_dtypes.bfloat16)


def sine(value):
    turns = jnp.round(value * (1.0 / math.pi))
    rest = value - turns * 3.140625
    rest = rest - turns * 9.67502593994140625e-4
    rest = rest - turns * 1.509957990978376432e-7
    parity = turns - 2.0 * jnp.floor(turns * 0.5)
    square = rest * rest
    poly = -2.3889859e-08 * square + 2.7525562e-06
    poly = poly * square - 0.00019840874
    poly = poly * square + 0.0083333310
    poly = poly * square - 0.16666667
    signed = rest - 2.0 * parity * rest
    return signed + signed * (square * poly)


def pieces(value, count):
    parts = []
    for _ in range(count):
        part = value.astype(jnp.bfloat16).astype(jnp.float32)
        parts.append(part)
        value = value - part
    return parts


LEFT_ORDER, RIGHT_ORDER = (0, 1, 0, 1, 0, 2), (0, 0, 1, 1, 2, 0)


def stacked(parts, order):
    return jnp.concatenate([parts[index] for index in order], axis=0).astype(jnp.bfloat16)


def stacked_dot(left, right):
    return lax.dot_general(
        left, right, (((0,), (0,)), ((), ())), preferred_element_type=jnp.float32
    )


def weighted(terms):
    total = None
    for factor, value in terms:
        if abs(factor) < 1e-9:
            continue
        if abs(factor - 1.0) < 1e-9:
            total = value if total is None else total + value
        elif abs(factor + 1.0) < 1e-9:
            total = -value if total is None else total - value
        else:
            part = value * factor
            total = part if total is None else total + part
    return total


def sections(load, store, blocks):
    half = blocks // 2
    x = [load(a).astype(jnp.float32) for a in range(blocks)]
    plus = {a: x[a] + x[blocks - a] for a in range(1, half)}
    minus = {a: x[a] - x[blocks - a] for a in range(1, half)}
    for c in range(blocks + 1):
        step = math.pi * c / blocks
        even = c % 2 == 0
        on_cos, on_sin = (plus, minus) if even else (minus, plus)
        middle = [(math.cos(step * half), x[half])] if even else []
        real = weighted([(1.0, x[0])] + middle + [(math.cos(step * a), on_cos[a]) for a in on_cos])
        store(c, 0, real.astype(jnp.bfloat16))
        if 0 < c < blocks:
            middle = [] if even else [(-math.sin(step * half), x[half])]
            imag = weighted(middle + [(-math.sin(step * a), on_sin[a]) for a in on_sin])
            store(c, 1, imag.astype(jnp.bfloat16))


def joined(load, store, blocks, factor):
    half = blocks // 2
    real = [load(c, 0) * (factor if c in (0, blocks) else 2.0 * factor) for c in range(blocks + 1)]
    imag = {c: load(c, 1) * (2.0 * factor) for c in range(1, blocks)}
    for a in range(half + 1):
        step = math.pi * a / blocks
        even_cos = weighted([(math.cos(step * c), real[c]) for c in range(0, blocks + 1, 2)])
        odd_cos = weighted([(math.cos(step * c), real[c]) for c in range(1, blocks + 1, 2)])
        even_sin = weighted([(math.sin(step * c), imag[c]) for c in range(2, blocks, 2)])
        odd_sin = weighted([(math.sin(step * c), imag[c]) for c in range(1, blocks, 2)])
        both = even_cos if odd_sin is None else even_cos - odd_sin
        turn = None
        if odd_cos is not None and even_sin is not None:
            turn = odd_cos - even_sin
        elif odd_cos is not None:
            turn = odd_cos
        elif even_sin is not None:
            turn = -even_sin
        store(a, (both if turn is None else both + turn).astype(jnp.bfloat16))
        if 0 < a < half:
            store(blocks - a, (both if turn is None else both - turn).astype(jnp.bfloat16))


def partner(me, mask, count):
    total, bit = 0, 1
    while bit < count:
        digit, flip = (me // bit) % 2, (mask // bit) % 2
        total = total + bit * (digit + flip - 2 * digit * flip)
        bit *= 2
    return total


def layer_kernel(
    blocks,
    span,
    own,
    signal_hbm,
    gate_in_hbm,
    gate_out_hbm,
    features_hbm,
    pos_weight_hbm,
    pos_bias_hbm,
    inner_weight_hbm,
    inner_bias_hbm,
    frequency_hbm,
    out_weight_hbm,
    decay_rates_hbm,
    skip_gain_hbm,
    forward_hbm,
    inverse_hbm,
    out,
    signal,
    gate_in,
    gate_out,
    features,
    pos_weight,
    pos_bias,
    inner_weight,
    inner_bias,
    frequency,
    weight,
    decay,
    skip_gain,
    forward,
    inverse,
    staged,
    wide_weight,
    gated,
    inbox,
    outbox,
    returned,
    hidden,
    taps,
    tap_rows,
    filt,
    data_rows,
    back,
    load_sem,
    leave_sem,
    send_sem,
    recv_sem,
):
    me = lax.axis_index("seq")
    chunks = own // LANES
    length = blocks * span
    far_first = list(range(blocks - 1, 0, -1))
    near_first = far_first[blocks // 2 :] + far_first[: blocks // 2]
    odd = lax.axis_index("grp") % 2
    peers = [partner(me, a + (b - a) * odd, blocks) for a, b in zip(near_first, far_first)]

    barrier = pltpu.get_barrier_semaphore()
    for peer in peers:
        pl.semaphore_signal(
            barrier, inc=1, device_id={"seq": peer}, device_id_type=pl.DeviceIdType.MESH
        )
    mine = pl.ds(pl.multiple_of(me * own, LANES), own)
    pairs = [
        (signal_hbm, signal),
        (gate_in_hbm, gate_in),
        (features_hbm, features),
        (pos_weight_hbm, pos_weight),
        (pos_bias_hbm, pos_bias),
        (frequency_hbm, frequency),
        (inner_weight_hbm, inner_weight),
        (inner_bias_hbm, inner_bias),
        (out_weight_hbm.at[:, mine], weight),
        (decay_rates_hbm.at[:, mine], decay),
        (forward_hbm, forward),
        (inverse_hbm, inverse),
        (gate_out_hbm, gate_out),
        (skip_gain_hbm, skip_gain),
    ]
    loads = [
        pltpu.make_async_copy(source, target, load_sem.at[index])
        for index, (source, target) in enumerate(pairs)
    ]
    for copy in loads:
        copy.start()

    for copy in loads[:2]:
        copy.wait()
    def gate(chunk):
        for owner in range(blocks):
            columns = pl.ds(owner * own + chunk * LANES, LANES)
            gated[owner, chunk] = (
                gate_in[0, :, columns].astype(jnp.float32)
                * signal[0, :, columns].astype(jnp.float32)
            ).astype(jnp.bfloat16)
        inbox[chunk, me] = gated[me, chunk]

    gate(0)
    pl.semaphore_wait(barrier, len(peers))

    def exchange(phase, chunk, source_of, target):
        copies = []
        for slot, peer in enumerate(peers):
            copy = pltpu.make_async_remote_copy(
                src_ref=source_of(peer),
                dst_ref=target.at[chunk, me],
                send_sem=send_sem.at[phase, chunk, slot],
                recv_sem=recv_sem.at[phase, chunk, slot],
                device_id={"seq": peer},
                device_id_type=pl.DeviceIdType.MESH,
            )
            copy.start()
            copies.append(copy)
        return copies

    def depart(chunk):
        return exchange(0, chunk, lambda peer: gated.at[peer, chunk], inbox)

    incoming = [depart(0)]
    for chunk in range(1, chunks):
        gate(chunk)

    order = frequency.shape[1]
    diagonal = lax.broadcasted_iota(jnp.int32, (order, order), 0) == lax.broadcasted_iota(
        jnp.int32, (order, order), 1
    )

    def as_column(row):
        return jnp.sum(jnp.where(diagonal, row, 0.0), axis=1, keepdims=True)

    def layer(left, right, bias):
        return sine(rate * (stacked_dot(left, right) + as_column(bias)))

    for copy in loads[2:10]:
        copy.wait()
    rate = as_column(frequency[...])
    wide_weight[...] = jnp.zeros_like(wide_weight)
    wide_weight[: pos_weight.shape[0], :] = pos_weight[...]
    left = stacked(pieces(wide_weight[...], 3), LEFT_ORDER)
    hidden[...] = layer(left, features[...], pos_bias[...])
    for index in range(inner_weight.shape[0]):
        left = stacked(pieces(inner_weight[index], 3), LEFT_ORDER)
        right = stacked(pieces(hidden[...], 3), RIGHT_ORDER)
        hidden[...] = layer(left, right, inner_bias[pl.ds(index, 1), :])
    right = stacked(pieces(weight[...], 2), (0, 0, 1, 1))
    energy = jnp.zeros((1, own), jnp.float32)
    for a in range(blocks):
        place = lax.broadcasted_iota(jnp.int32, (span, own), 0) + a * span
        moment = place.astype(jnp.float32) / float(length - 1)
        left = stacked(pieces(hidden[:, a * span : (a + 1) * span], 2), (0, 1, 0, 1))
        raw = stacked_dot(left, right) * (jnp.exp(-moment * decay[...]) + FLOOR_SHIFT)
        energy = energy + jnp.sum(raw * raw, axis=0, keepdims=True)
        taps[a] = raw.astype(jnp.bfloat16)
    scale = lax.rsqrt(energy + EPSILON)

    for chunk in range(1, chunks):
        for copy in incoming[chunk - 1]:
            copy.wait_send()
        incoming.append(depart(chunk))

    group = 16

    def tap_section(step, carry):
        rows = pl.ds(pl.multiple_of(step * group, group), group)

        def store(c, part, value):
            tap_rows[c, part, rows, :] = value

        sections(lambda a: taps[a, rows, :], store, blocks)
        return carry

    lax.fori_loop(0, span // group, tap_section, 0)
    for copy in loads[10:12]:
        copy.wait()

    def spectrum(c, rows):
        if c in (0, blocks):
            table, data = forward[c, :, :span], rows[0]
        else:
            table, data = forward[c], jnp.concatenate([rows[0], rows[1]], axis=0)
        return jnp.dot(table, data, preferred_element_type=jnp.float32)

    for c in range(blocks + 1):
        filt[c] = spectrum(c, tap_rows.at[c]) * scale

    outgoing = []
    for chunk in range(chunks):
        for copy in incoming[chunk]:
            copy.wait_recv()

        def data_section(step, carry):
            rows = pl.ds(pl.multiple_of(step * group, group), group)

            def store(c, part, value):
                data_rows[c, part, rows, :] = value

            sections(lambda a: inbox[chunk, a, rows, :], store, blocks)
            return carry

        lax.fori_loop(0, span // group, data_section, 0)
        lanes = slice(chunk * LANES, (chunk + 1) * LANES)
        for c in range(blocks + 1):
            wave = spectrum(c, data_rows.at[c])
            wave_real, wave_imag = wave[:span], wave[span:]
            filt_real, filt_imag = filt[c, :span, lanes], filt[c, span:, lanes]
            product = jnp.concatenate(
                [
                    (wave_real * filt_real - wave_imag * filt_imag).astype(jnp.bfloat16),
                    (wave_real * filt_imag + wave_imag * filt_real).astype(jnp.bfloat16),
                ],
                axis=0,
            )
            if c in (0, blocks):
                back[c, :span] = jnp.dot(
                    inverse[c, :span, :], product, preferred_element_type=jnp.float32
                )
            else:
                back[c] = jnp.dot(inverse[c], product, preferred_element_type=jnp.float32)

        def join_section(step, carry):
            small = 8

            def load(c, part):
                return back[c, pl.ds(pl.multiple_of(part * span + step * group, small), group), :]

            def store(a, value):
                outbox[chunk, a, pl.ds(pl.multiple_of(step * group, group), group), :] = value

            joined(load, store, blocks, 1.0 / (2 * length))
            return carry

        lax.fori_loop(0, span // group, join_section, 0)
        outgoing.append(
            exchange(1, chunk, lambda peer, chunk=chunk: outbox.at[chunk, peer], returned)
        )

    def finish(chunk, slot, owner, convolved):
        columns = pl.ds(pl.multiple_of(owner * own + chunk * LANES, LANES), LANES)
        staged[0, :, columns] = (
            gate_out[0, :, columns].astype(jnp.float32)
            * (
                convolved.astype(jnp.float32)
                + skip_gain[:, columns] * gated[owner, chunk].astype(jnp.float32)
            )
        ).astype(jnp.bfloat16)
        copy = pltpu.make_async_copy(
            staged.at[:, :, columns], out.at[:, :, columns], leave_sem.at[chunk, slot]
        )
        copy.start()
        leaving.append(copy)

    leaving = []
    for copy in loads[12:]:
        copy.wait()
    for chunk in range(chunks):
        finish(chunk, 0, me, outbox[chunk, me])
    for chunk in range(chunks):
        for slot, (peer, copy) in enumerate(zip(peers, outgoing[chunk])):
            copy.wait_recv()
            finish(chunk, slot + 1, peer, returned[chunk, peer])
    for copy in leaving:
        copy.wait()
    for copies in incoming[-1:] + outgoing:
        for copy in copies:
            copy.wait_send()


def fused(
    signal,
    gate_in,
    gate_out,
    pos_weight,
    pos_bias,
    inner_weight,
    inner_bias,
    frequency,
    out_weight,
    decay_rates,
    skip_gain,
):
    blocks = lax.axis_size("seq")
    span, width = signal.shape[1], signal.shape[2]
    own = width // blocks
    chunks = own // LANES
    length = span * blocks
    order = frequency.shape[0]
    forward, inverse = row_matrices(blocks, span)
    features = position_features(length, pos_weight.shape[0])
    hbm = pl.BlockSpec(memory_space=pltpu.HBM)
    bf16, f32 = jnp.bfloat16, jnp.float32
    operands = (
        signal,
        gate_in,
        gate_out,
        jnp.asarray(features),
        pos_weight,
        pos_bias.reshape(1, -1),
        inner_weight,
        inner_bias,
        frequency.reshape(1, -1),
        out_weight,
        decay_rates.reshape(1, -1),
        skip_gain.reshape(1, -1),
        jnp.asarray(forward),
        jnp.asarray(inverse),
    )
    shapes = [operand.shape for operand in operands]
    shapes[9], shapes[10] = (order, own), (1, own)
    locals_ = [pltpu.VMEM(shape, operand.dtype) for shape, operand in zip(shapes, operands)]
    return pl.pallas_call(
        functools.partial(layer_kernel, blocks, span, own),
        out_shape=jax.ShapeDtypeStruct(signal.shape, bf16),
        in_specs=[hbm] * len(operands),
        out_specs=hbm,
        scratch_shapes=[
            *locals_,
            pltpu.VMEM(signal.shape, bf16),
            pltpu.VMEM((padded(pos_weight.shape[0]), order), f32),
            pltpu.VMEM((blocks, chunks, span, LANES), bf16),
            pltpu.VMEM((chunks, blocks, span, LANES), bf16),
            pltpu.VMEM((chunks, blocks, span, LANES), bf16),
            pltpu.VMEM((chunks, blocks, span, LANES), bf16),
            pltpu.VMEM((order, length), f32),
            pltpu.VMEM((blocks, span, own), bf16),
            pltpu.VMEM((blocks + 1, 2, span, own), bf16),
            pltpu.VMEM((blocks + 1, 2 * span, own), f32),
            pltpu.VMEM((blocks + 1, 2, span, LANES), bf16),
            pltpu.VMEM((blocks + 1, 2 * span, LANES), f32),
            pltpu.SemaphoreType.DMA((len(operands),)),
            pltpu.SemaphoreType.DMA((chunks, blocks)),
            pltpu.SemaphoreType.DMA((2, chunks, blocks)),
            pltpu.SemaphoreType.DMA((2, chunks, blocks)),
        ],
        compiler_params=pltpu.CompilerParams(
            collective_id=0, has_side_effects=True, vmem_limit_bytes=62 * MIB
        ),
        name="hyena_layer",
    )(*operands)


def unit_angle(index, period):
    return (index % period).astype(jnp.float32) * (TWO_PI / period)


def section_tables(row_ids, col_ids, period):
    angle = unit_angle(row_ids[:, None] * col_ids[None, :], period)
    return (jnp.cos(angle).astype(jnp.bfloat16), jnp.sin(angle).astype(jnp.bfloat16))


def filter_hidden(positions, total, pos_weight, pos_bias, inner_weight, inner_bias, frequency):
    band_count = (pos_weight.shape[0] - 1) // 2
    position_f = positions.astype(jnp.float32)
    moments = position_f / (total - 1)
    phases = position_f * (TWO_PI / total)
    tone_list = jnp.linspace(0.0001, band_count - 1, band_count).astype(jnp.float32)
    angles = tone_list[:, None] * phases[None, :]
    features = jnp.concatenate([moments[None, :], jnp.cos(angles), -jnp.sin(angles)], axis=0)
    hidden = jnp.sin(
        frequency[:, None]
        * (jnp.dot(pos_weight.T, features, precision=HIGHEST) + pos_bias[:, None])
    )
    for layer_index in range(inner_weight.shape[0]):
        hidden = jnp.sin(
            frequency[:, None]
            * (
                jnp.dot(inner_weight[layer_index].T, hidden, precision=HIGHEST)
                + inner_bias[layer_index][:, None]
            )
        )
    return (hidden, moments)


def plain(
    signal,
    gate_in,
    gate_out,
    pos_weight,
    pos_bias,
    inner_weight,
    inner_bias,
    frequency,
    out_weight,
    decay_rates,
    skip_gain,
):
    blocks = lax.axis_size("seq")
    block_id = lax.axis_index("seq")
    span = signal.shape[1]
    width = signal.shape[2]
    rows_freq = 2 * blocks
    length = span * blocks
    period = 2 * length
    gated = (gate_in[0].astype(jnp.float32) * signal[0].astype(jnp.float32)).astype(jnp.bfloat16)
    fwd_cos, fwd_sin = section_tables(
        jnp.arange(rows_freq, dtype=jnp.int32), jnp.arange(blocks, dtype=jnp.int32), rows_freq
    )
    back_cos, back_sin = section_tables(
        jnp.arange(blocks, dtype=jnp.int32), jnp.arange(rows_freq, dtype=jnp.int32), rows_freq
    )
    column_ids = jnp.arange(span, dtype=jnp.int32)
    own = width // blocks
    lanes = lax.all_to_all(gated.T, "seq", split_axis=0, concat_axis=1, tiled=True)
    own_weight = lax.dynamic_slice_in_dim(out_weight, block_id * own, own, 1)
    own_decay = lax.dynamic_slice_in_dim(decay_rates, block_id * own, own, 0)
    hidden, moments = filter_hidden(
        jnp.arange(length, dtype=jnp.int32),
        length,
        pos_weight,
        pos_bias,
        inner_weight,
        inner_bias,
        frequency,
    )
    shaped = jnp.dot(own_weight.T, hidden, precision=HIGHEST) * (
        jnp.exp(-own_decay[:, None] * moments[None, :]) + FLOOR_SHIFT
    )
    own_scale = lax.rsqrt(jnp.sum(shaped * shaped, axis=1) + EPSILON)
    own_taps = shaped.astype(jnp.bfloat16)

    def first_local(source):
        cube = source.reshape(own, blocks, span)
        real_part = jnp.einsum(
            "ca,oab->cob", fwd_cos, cube, preferred_element_type=jnp.float32
        ).astype(jnp.bfloat16)
        imag_part = (
            -jnp.einsum("ca,oab->cob", fwd_sin, cube, preferred_element_type=jnp.float32)
        ).astype(jnp.bfloat16)
        return (real_part, imag_part)

    data_real, data_imag = first_local(lanes)
    taps_real, taps_imag = first_local(own_taps)
    group = 16
    turns = rows_freq // group

    def grouped(array):
        return array.reshape(turns, group, own, span)

    def row_group(pieces):
        row_real, row_imag, tap_real, tap_imag, row_ids = pieces
        wave_ids = row_ids[:, None] + rows_freq * column_ids[None, :]
        angle = unit_angle(wave_ids[:, :, None] * column_ids[None, None, :], period)
        cosines = jnp.cos(angle).astype(jnp.bfloat16)
        sines = jnp.sin(angle).astype(jnp.bfloat16)

        def spectrum_of(part_real, part_imag):
            spec_real = jnp.einsum(
                "rdb,rob->rod", cosines, part_real, preferred_element_type=jnp.float32
            ) + jnp.einsum("rdb,rob->rod", sines, part_imag, preferred_element_type=jnp.float32)
            spec_imag = jnp.einsum(
                "rdb,rob->rod", cosines, part_imag, preferred_element_type=jnp.float32
            ) - jnp.einsum("rdb,rob->rod", sines, part_real, preferred_element_type=jnp.float32)
            return (spec_real, spec_imag)

        wave_real, wave_imag = spectrum_of(row_real, row_imag)
        spec_real, spec_imag = spectrum_of(tap_real, tap_imag)
        filt_real = spec_real.astype(jnp.bfloat16).astype(jnp.float32)
        filt_imag = spec_imag.astype(jnp.bfloat16).astype(jnp.float32)
        lane_scale = own_scale[None, :, None]
        prod_real = ((wave_real * filt_real - wave_imag * filt_imag) * lane_scale).astype(
            jnp.bfloat16
        )
        prod_imag = ((wave_real * filt_imag + wave_imag * filt_real) * lane_scale).astype(
            jnp.bfloat16
        )
        back_real = jnp.einsum(
            "rdb,rod->rob", cosines, prod_real, preferred_element_type=jnp.float32
        ) - jnp.einsum("rdb,rod->rob", sines, prod_imag, preferred_element_type=jnp.float32)
        back_imag = jnp.einsum(
            "rdb,rod->rob", cosines, prod_imag, preferred_element_type=jnp.float32
        ) + jnp.einsum("rdb,rod->rob", sines, prod_real, preferred_element_type=jnp.float32)
        return (back_real.astype(jnp.bfloat16), back_imag.astype(jnp.bfloat16))

    row_list = jnp.arange(rows_freq, dtype=jnp.int32).reshape(turns, group)
    back_real, back_imag = lax.map(
        row_group,
        (grouped(data_real), grouped(data_imag), grouped(taps_real), grouped(taps_imag), row_list),
    )
    back_real = back_real.reshape(rows_freq, own, span)
    back_imag = back_imag.reshape(rows_freq, own, span)
    local_conv = (
        jnp.einsum("ac,cob->oab", back_cos, back_real, preferred_element_type=jnp.float32)
        - jnp.einsum("ac,cob->oab", back_sin, back_imag, preferred_element_type=jnp.float32)
    ) * (1.0 / period)
    returned = lax.all_to_all(
        local_conv.reshape(own, length).astype(jnp.bfloat16),
        "seq",
        split_axis=1,
        concat_axis=0,
        tiled=True,
    ).astype(jnp.float32)
    convolved_rows = returned.T
    mixed = gate_out[0].astype(jnp.float32) * (
        convolved_rows + skip_gain[None, :] * gated.astype(jnp.float32)
    )
    return mixed.astype(jnp.bfloat16)[None]


def fits_kernel(blocks, span, width):
    own = width // blocks
    power = blocks >= 4 and blocks & (blocks - 1) == 0
    return power and span == LANES and own > 0 and own % LANES == 0


def per_device(signal, *rest):
    if fits_kernel(lax.axis_size("seq"), signal.shape[1], signal.shape[2]):
        return fused(signal, *rest)
    return plain(signal, *rest)


def solution(mesh):
    return jax.shard_map(
        per_device,
        mesh=mesh,
        in_specs=(
            P("grp", "seq", None),
            P("grp", "seq", None),
            P("grp", "seq", None),
            P(),
            P(),
            P(),
            P(),
            P(),
            P(),
            P(),
            P(),
        ),
        out_specs=P("grp", "seq", None),
        check_vma=False,
    )
```
